32 devices in a mesh: seq: 16 (over z, y, x), doc: 2 (over core).
Axes of the slice: x: 2, y: 2, z: 4, core: 2. Of those that a mesh axis runs over, the one named last changes fastest.
Arguments:
- conv_input: bfloat16 [4096, 4352], P(('doc', 'seq')), parts along dimension 0, may hold values from -6 to 6
- gate_input: bfloat16 [4096, 4096], P(('doc', 'seq')), parts along dimension 0, may hold values from -6 to 6
- step_input: bfloat16 [4096, 64], P(('doc', 'seq')), parts along dimension 0, may hold values from -1.1 to 2.9
- conv_weight: float32 [4, 4352], replicated, may hold values from -3 to 3
- convolution_bias: float32 [4352], replicated, may hold values from -0.5 to 0.5
- step_bias: float32 [64], replicated, may hold values from -12 to -2, as said below
- decay_log: float32 [64], replicated, may hold values from -3.3 to -1, as said below
- skip_gain: float32 [64], replicated, may hold values from 0.5 to 2
- norm_gain: float32 [4096], replicated, may hold values from 0.5 to 1.5
Outputs:
- normed: bfloat16 [4096, 4096], P(('doc', 'seq')), parts along dimension 0
The draws below stay inside these ranges and needn't reach their ends.
There are 2 independent parts, one for each index of `doc`. The reference program is written for one: setup_inputs(seed, part) draws one part's arguments, and reference() takes and returns one part's arrays. A program takes and returns all parts, laid end to end along the dimension named above; an argument that names none is the same for every part. Nothing has to cross between parts.
Inputs may be any that keep to these rules, and one draw needn't show every extreme that they name: `decay_log`: one value a head. `step_bias`: one value a head.
All inputs are finite; a program needn't handle non-finite values.
Results may differ from the reference program's by a relative error of at most 0.0051.
Values may be sent and summed in bfloat16 or wider, within the bound.
A program may use at most 64 MiB of HBM per device.

```python
import math
import jax
import jax.numpy as jnp
from jax import lax

HEADDIM = 64
STATE = 128
HEADS = 64
TAPS = 4
STRETCH = 256
TOK_DEV = 128
INNER = 4096
CONV = 4352
DOCUMENT_LENGTH = 2048


def head_plan(key):
    plan_key = jax.random.fold_in(key, 11)
    kind_key, slow_key, fast_key = jax.random.split(plan_key, 3)
    share = 0.5
    fast = jax.random.uniform(kind_key, (HEADS,)) < share
    slow_rate = jnp.exp(jax.random.uniform(slow_key, (HEADS,), minval=math.log(0.15), maxval=math.log(0.6))) / 4.0
    span = jax.random.uniform(fast_key, (HEADS,), minval=30.0, maxval=50.0)
    magnitude = jnp.where(fast, 10.0 / span, slow_rate)
    base_step = jnp.where(fast, 0.1, 4.0 / DOCUMENT_LENGTH)
    return (magnitude, base_step)


def draw_decay_log(key, part):
    magnitude, base_step = head_plan(key)
    return jnp.log(magnitude).astype(jnp.float32)


def draw_step_bias(key, part):
    magnitude, base_step = head_plan(key)
    return jnp.log(jnp.expm1(base_step)).astype(jnp.float32)


def draw_step_input(key, part):
    block_random_key, memory_cell_key, pulse_random_key = jax.random.split(jax.random.fold_in(key, 23), 3)
    block_count = DOCUMENT_LENGTH // TOK_DEV
    block_scale = jax.random.uniform(block_random_key, (block_count, 1, HEADS), minval=math.log(0.5), maxval=math.log(1.6))
    cell = jax.random.uniform(memory_cell_key, (block_count, TOK_DEV, HEADS), minval=math.log(0.7), maxval=math.log(1.4))
    raw_steps = (block_scale + cell).reshape(DOCUMENT_LENGTH, HEADS)
    position_marks = jax.random.randint(pulse_random_key, (3,), 0, DOCUMENT_LENGTH)
    hits = jnp.any(jnp.arange(DOCUMENT_LENGTH)[:, None] == position_marks[None, :], axis=1)
    raw_steps = raw_steps + jnp.where(hits, 2.0, 0.0)[:, None]
    return raw_steps.astype(jnp.bfloat16)


def shard_levels(stream_key, extent, cuts, low, top_value):
    gain = 1.0
    for dim, parts in cuts:
        heights = jax.random.uniform(jax.random.fold_in(jax.random.fold_in(stream_key, 6), dim), (parts,), jnp.float32, low / len(cuts), top_value / len(cuts))
        gain = gain * jnp.repeat(jnp.exp(heights), extent[dim] // parts).reshape((-1,) + (1,) * (len(extent) - 1 - dim))
    return gain


def gaussian(rng, extent, deviation, most, shards=(), dtype=jnp.bfloat16):
    factor_of = shard_levels(rng, extent, shards, -0.22, 0.18) if shards else 1.0
    values = jax.random.normal(rng, extent, jnp.float32) * deviation * factor_of
    return jnp.minimum(jnp.maximum(values, -most), most).astype(dtype)


def setup_inputs(seed: int = 0, part: int = 0) -> dict:
    arg_keys = jax.random.split(jax.random.key(seed), 10)
    own_keys = jax.random.split(jax.random.fold_in(arg_keys[9], part), 10)
    return {
        "conv_input": gaussian(own_keys[0], (DOCUMENT_LENGTH, CONV), 1.0, 6.0, ((0, 16),)),
        "gate_input": gaussian(own_keys[1], (DOCUMENT_LENGTH, INNER), 1.0, 6.0, ((0, 16),)),
        "step_input": draw_step_input(jax.random.fold_in(jax.random.fold_in(arg_keys[9], part), 71), part),
        "conv_weight": gaussian(arg_keys[3], (TAPS, CONV), TAPS ** -0.5, 3.0, (), jnp.float32),
        "convolution_bias": jnp.clip(jax.random.uniform(arg_keys[4], (CONV,), jnp.float32, -0.5, 0.5), -0.5, 0.5),
        "step_bias": draw_step_bias(jax.random.fold_in(arg_keys[9], 71), part),
        "decay_log": draw_decay_log(jax.random.fold_in(arg_keys[9], 71), part),
        "skip_gain": jnp.clip(jnp.exp(jax.random.uniform(arg_keys[7], (HEADS,), jnp.float32, math.log(0.5), math.log(2.0))), 0.5, 2.0),
        "norm_gain": jnp.clip(1.0 + 0.1 * jax.random.normal(arg_keys[8], (INNER,), jnp.float32), 0.5, 1.5),
    }


def gated_norm(mixed_out, gate_input, norm_gain):
    gated = mixed_out.astype(jnp.float32) * jax.nn.silu(gate_input.astype(jnp.float32))
    spread = lax.optimization_barrier(jnp.mean(gated * gated, axis=-1, keepdims=True))
    return (gated * lax.rsqrt(spread + 1e-05) * norm_gain[None, :]).astype(jnp.bfloat16)

def reference(conv_input, gate_input, step_input, conv_weight, convolution_bias, step_bias, decay_log, skip_gain, norm_gain):
    highest = lax.Precision.HIGHEST
    row_count = conv_input.shape[0]
    tap_count = conv_weight.shape[0]
    padded = jnp.pad(conv_input.astype(jnp.float32), ((tap_count - 1, 0), (0, 0)))
    mixed = convolution_bias[None, :]
    for offset in range(tap_count):
        mixed = mixed + conv_weight[offset][None, :] * padded[offset:offset + row_count]
    activated = jax.nn.silu(mixed).astype(jnp.bfloat16)
    inner_width = HEADS * HEADDIM
    values = activated[:, :inner_width].astype(jnp.float32).reshape(row_count, HEADS, HEADDIM)
    b_rows = activated[:, inner_width:inner_width + STATE].astype(jnp.float32)
    c_rows = activated[:, inner_width + STATE:].astype(jnp.float32)
    step_size = jax.nn.softplus(step_input.astype(jnp.float32) + step_bias[None, :])
    decay_rate = -jnp.exp(decay_log)
    blocks = row_count // STRETCH
    lower = jnp.arange(STRETCH)[:, None] >= jnp.arange(STRETCH)[None, :]

    def advance(carried, pieces):
        block_values, block_step_sizes, block_b, block_c = pieces
        within = jnp.cumsum(block_step_sizes * decay_rate[None, :], axis=0)
        diffs = jnp.where(lower[None], within.T[:, :, None] - within.T[:, None, :], -jnp.inf)
        scores = jnp.dot(block_c, block_b.T, precision=highest, preferred_element_type=jnp.float32)
        mixing = jnp.exp(diffs) * scores[None] * block_step_sizes.T[:, None, :]
        inside = jnp.einsum('hts,shp->thp', mixing, block_values, precision=highest)
        outside = jnp.exp(within)[:, :, None] * jnp.einsum('tn,hpn->thp', block_c, carried, precision=highest)
        tail = jnp.exp(within[-1][None, :] - within) * block_step_sizes
        added = jnp.einsum('sh,shp,sn->hpn', tail, block_values, block_b, precision=highest)
        updated = jnp.exp(within[-1])[:, None, None] * carried + added
        return (updated, inside + outside)
    start = jnp.zeros((HEADS, HEADDIM, STATE), jnp.float32)
    final_state, outputs = lax.scan(advance, start, (values.reshape(blocks, STRETCH, HEADS, HEADDIM), step_size.reshape(blocks, STRETCH, HEADS), b_rows.reshape(blocks, STRETCH, STATE), c_rows.reshape(blocks, STRETCH, STATE)))
    result = outputs.reshape(row_count, HEADS, HEADDIM) + skip_gain[None, :, None] * values
    mixed_out = result.astype(jnp.bfloat16).reshape(row_count, inner_width)
    return gated_norm(mixed_out, gate_input, norm_gain)
```

```python
import functools
import jax
import jax.numpy as jnp
from jax import lax
from jax.experimental import pallas as pl
from jax.experimental.pallas import tpu as pltpu
from jax.sharding import PartitionSpec as P

HEADDIM = 64
STATE = 128
HEADS = 64
GROUP = 4
PARTS = 4
EXTRA = 16
MESH = pl.DeviceIdType.MESH


def shifted(value, axis, steps):
    count = lax.axis_size(axis)
    initial, last = (max(0, -steps), min(count, count - steps))
    return lax.ppermute(value, axis, [(source, source + steps) for source in range(initial, last)])


def convolve(conv_input, conv_weight, convolution_bias):
    tap_count = conv_weight.shape[0]
    row_count = conv_input.shape[0]
    earlier = shifted(conv_input[row_count - (tap_count - 1) :], "seq", 1)
    padded = jnp.concatenate([earlier, conv_input], axis=0).astype(jnp.float32)
    mixed = convolution_bias[None, :]
    for offset in range(tap_count):
        mixed = mixed + conv_weight[offset][None, :] * padded[offset : offset + row_count]
    return jax.nn.silu(mixed).astype(jnp.bfloat16)


def prefix_kernel(
    count, group, s_ref, f_ref, got, ein, eout, fsend, gsum,
    send_a, recv_a, send_c, recv_c, send_f, recv_f,
):
    rows = ein.shape[0]
    width = ein.shape[1]
    part = width // PARTS
    planes = count // group
    me = lax.axis_index("seq")
    mine = lax.rem(me, group)
    plane = me // group
    base = plane * group
    has_prev = plane > 0
    has_next = plane < planes - 1
    before = jnp.maximum(me - group, 0)
    after = jnp.minimum(me + group, count - 1)

    barrier = pltpu.get_barrier_semaphore()
    for step in range(1, group):
        other = base + lax.rem(mine + step, group)
        pl.semaphore_signal(barrier, inc=1, device_id={"seq": other}, device_id_type=MESH)

    @pl.when(has_prev)
    def _():
        pl.semaphore_signal(barrier, inc=1, device_id={"seq": before}, device_id_type=MESH)

    @pl.when(has_next)
    def _():
        pl.semaphore_signal(barrier, inc=1, device_id={"seq": after}, device_id_type=MESH)

    peers = group - 1 + jnp.minimum(plane, 1) + jnp.minimum(planes - 1 - plane, 1)
    pl.semaphore_wait(barrier, peers)

    def share(step):
        member = lax.rem(mine + step, group)
        return pltpu.make_async_remote_copy(
            src_ref=s_ref.at[:, pl.ds(pl.multiple_of(member * width, width), width)],
            dst_ref=got.at[step],
            send_sem=send_a.at[step],
            recv_sem=recv_a.at[step],
            device_id={"seq": base + member},
            device_id_type=MESH,
        )

    def chain(k):
        columns = pl.ds(k * part, part)
        return pltpu.make_async_remote_copy(
            src_ref=eout.at[:, columns],
            dst_ref=ein.at[:, columns],
            send_sem=send_c.at[k],
            recv_sem=recv_c.at[k],
            device_id={"seq": after},
            device_id_type=MESH,
        )

    def back(step, k):
        member = lax.rem(mine + step, group)
        own = pl.ds(pl.multiple_of(mine * width + k * part, part), part)
        return pltpu.make_async_remote_copy(
            src_ref=fsend.at[step, :, pl.ds(k * part, part)],
            dst_ref=f_ref.at[:, own],
            send_sem=send_f.at[step, k],
            recv_sem=recv_f.at[step, k],
            device_id={"seq": base + member},
            device_id_type=MESH,
        )

    for step in range(1, group):
        share(step).start()
    got[0] = s_ref[:, pl.ds(pl.multiple_of(mine * width, width), width)]
    for step in range(1, group):
        share(step).wait_recv()

    slots = [lax.rem(mine - i + group, group) for i in range(group)]
    marks = []
    for k in range(PARTS):
        columns = pl.ds(k * part, part)
        running = jnp.zeros((rows, part), jnp.float32)
        level = jnp.zeros((1, part), jnp.float32)
        levels = [level]
        for i in range(group):
            tail = got[slots[i], rows : rows + EXTRA, columns].astype(jnp.float32)
            step_log = tail[0:1] + tail[1:2] + tail[2:3]
            running = jnp.exp(step_log) * running + got[slots[i], :rows, columns].astype(jnp.float32)
            gsum[i, :, columns] = running
            level = level + step_log
            levels.append(level)
        marks.append(levels)

    for k in range(PARTS):
        columns = pl.ds(k * part, part)
        levels = marks[k]

        @pl.when(has_prev)
        def _():
            chain(k).wait_recv()

        @pl.when(jnp.logical_not(has_prev))
        def _():
            ein[:, columns] = jnp.zeros((rows, part), jnp.bfloat16)

        entering = ein[:, columns].astype(jnp.float32)

        @pl.when(has_next)
        def _():
            eout[:, columns] = (jnp.exp(levels[group]) * entering + gsum[group - 1, :, columns]).astype(jnp.bfloat16)
            chain(k).start()

        for j in range(group):
            if j == 0:
                value = entering
            else:
                value = jnp.exp(levels[j]) * entering + gsum[j - 1, :, columns]
            fsend[lax.rem(j - mine + group, group), :, columns] = value.astype(jnp.bfloat16)
        for step in range(1, group):
            back(step, k).start()
        own = pl.ds(pl.multiple_of(mine * width + k * part, part), part)
        f_ref[:, own] = fsend[0, :, columns]

    for step in range(1, group):
        share(step).wait_send()
    for k in range(PARTS):
        @pl.when(has_next)
        def _():
            chain(k).wait_send()

        for step in range(1, group):
            back(step, k).wait_send()
            source = lax.rem(mine - step + group, group)
            landed = pl.ds(pl.multiple_of(source * width + k * part, part), part)
            pltpu.make_async_remote_copy(
                src_ref=fsend.at[step, :, pl.ds(k * part, part)],
                dst_ref=f_ref.at[:, landed],
                send_sem=send_f.at[step, k],
                recv_sem=recv_f.at[step, k],
                device_id={"seq": base + lax.rem(mine + step, group)},
                device_id_type=MESH,
            ).wait_recv()


def entering_states(packed):
    count = lax.axis_size("seq")
    group = GROUP if count % GROUP == 0 else 1
    rows = packed.shape[0] - EXTRA
    width = packed.shape[1] // group
    return pl.pallas_call(
        functools.partial(prefix_kernel, count, group),
        out_shape=jax.ShapeDtypeStruct((rows, packed.shape[1]), jnp.bfloat16),
        in_specs=[pl.BlockSpec(memory_space=pltpu.VMEM)],
        out_specs=pl.BlockSpec(memory_space=pltpu.VMEM),
        scratch_shapes=[
            pltpu.VMEM((group, rows + EXTRA, width), jnp.bfloat16),
            pltpu.VMEM((rows, width), jnp.bfloat16),
            pltpu.VMEM((rows, width), jnp.bfloat16),
            pltpu.VMEM((group, rows, width), jnp.bfloat16),
            pltpu.VMEM((group, rows, width), jnp.float32),
            pltpu.SemaphoreType.DMA((group,)),
            pltpu.SemaphoreType.DMA((group,)),
            pltpu.SemaphoreType.DMA((PARTS,)),
            pltpu.SemaphoreType.DMA((PARTS,)),
            pltpu.SemaphoreType.DMA((group, PARTS)),
            pltpu.SemaphoreType.DMA((group, PARTS)),
        ],
        compiler_params=pltpu.CompilerParams(
            collective_id=0, has_side_effects=True, vmem_limit_bytes=32 * 1024 * 1024
        ),
    )(packed)


def split(value):
    high = value.astype(jnp.bfloat16)
    low = (value - high.astype(jnp.float32)).astype(jnp.bfloat16)
    return high, low


def mix_kernel(act, entering, gate, cols, rows_ref, steps, skip, gain, out, mixed):
    tokens = act.shape[0]
    inner = entering.shape[1]
    block = 8 * HEADDIM
    b_rows = act[:, inner : inner + STATE]
    c_rows = act[:, inner + STATE : inner + 2 * STATE]
    scores = lax.dot_general(c_rows, b_rows, (((1,), (1,)), ((), ())), preferred_element_type=jnp.float32)
    lower = lax.broadcasted_iota(jnp.int32, (tokens, tokens), 0) >= lax.broadcasted_iota(jnp.int32, (tokens, tokens), 1)
    scores = jnp.where(lower, scores, 0.0)
    c_wide = c_rows.astype(jnp.float32)
    first = lax.broadcasted_iota(jnp.int32, (tokens, 2 * HEADDIM), 1) < HEADDIM

    def body(g, carry):
        for pair in range(4):
            columns = pl.ds(pl.multiple_of(g * block + pair * 128, 128), 128)
            x = act[:, columns]
            stacked = jnp.concatenate([x, entering[:, columns]], axis=0)
            halves = []
            for half in range(2):
                h = pair * 2 + half
                col = cols[g, :, h : h + 1]
                row = rows_ref[g, h : h + 1, :]
                inside = jnp.exp(jnp.where(lower, col - row, -1e30)) * scores * steps[g, h : h + 1, :]
                whole = jnp.concatenate([inside, jnp.exp(col) * c_wide], axis=1)
                high, low = split(whole)
                halves.append(
                    jnp.dot(high, stacked, preferred_element_type=jnp.float32)
                    + jnp.dot(low, stacked, preferred_element_type=jnp.float32)
                )
            result = jnp.where(first, halves[0], halves[1]) + skip[:, columns] * x.astype(jnp.float32)
            mixed[:, columns] = result.astype(jnp.bfloat16)
        return carry

    lax.fori_loop(0, inner // block, body, 0)

    def norm(r, carry):
        take = pl.ds(pl.multiple_of(r * 16, 16), 16)
        z = gate[take, :].astype(jnp.float32)
        gated = mixed[take, :].astype(jnp.float32) * (z / (1.0 + jnp.exp(-z)))
        spread = jnp.mean(gated * gated, axis=-1, keepdims=True)
        out[take, :] = (gated * lax.rsqrt(spread + 1e-05) * gain[...]).astype(jnp.bfloat16)
        return carry

    lax.fori_loop(0, tokens // 16, norm, 0)


def shards(
    conv_input, gate_input, step_input, conv_weight, convolution_bias,
    step_bias, decay_log, skip_gain, norm_gain,
):
    highest = lax.Precision.HIGHEST
    inner = HEADS * HEADDIM
    tokens = conv_input.shape[0]
    activated = convolve(conv_input, conv_weight, convolution_bias)
    step_size = jax.nn.softplus(step_input.astype(jnp.float32) + step_bias[None, :])
    rate = -jnp.exp(decay_log)
    lower = (jnp.arange(tokens)[:, None] >= jnp.arange(tokens)[None, :]).astype(jnp.float32)
    within = jnp.dot(lower, step_size * rate[None, :], precision=highest)
    ends = within[-1]
    tail = jnp.repeat(jnp.exp(ends[None, :] - within) * step_size, HEADDIM, axis=1)
    weighted = (tail * activated[:, :inner].astype(jnp.float32)).astype(jnp.bfloat16)
    state = lax.dot_general(
        activated[:, inner : inner + STATE], weighted, (((0,), (0,)), ((), ())),
        preferred_element_type=jnp.float32,
    ).astype(jnp.bfloat16)
    high = lax.reduce_precision(ends, 8, 7)
    middle = lax.reduce_precision(ends - high, 8, 7)
    low = lax.reduce_precision(ends - high - middle, 8, 7)
    logs = jnp.repeat(jnp.stack([high, middle, low]), HEADDIM, axis=1).astype(jnp.bfloat16)
    packed = jnp.concatenate([state, logs, jnp.zeros((EXTRA - 3, inner), jnp.bfloat16)], axis=0)
    entering = entering_states(packed)
    groups = HEADS // 8
    cols = jnp.transpose(within.reshape(tokens, groups, 8), (1, 0, 2))
    rows = jnp.transpose(within).reshape(groups, 8, tokens)
    steps = jnp.transpose(step_size).reshape(groups, 8, tokens)
    skip = jnp.repeat(skip_gain, HEADDIM)[None, :]
    return pl.pallas_call(
        mix_kernel,
        out_shape=jax.ShapeDtypeStruct((tokens, inner), jnp.bfloat16),
        in_specs=[pl.BlockSpec(memory_space=pltpu.VMEM)] * 8,
        out_specs=pl.BlockSpec(memory_space=pltpu.VMEM),
        scratch_shapes=[pltpu.VMEM((tokens, inner), jnp.bfloat16)],
        compiler_params=pltpu.CompilerParams(vmem_limit_bytes=32 * 1024 * 1024),
    )(activated, entering, gate_input, cols, rows, steps, skip, norm_gain[None, :])


def solution(mesh):
    in_specs = (
        P(("doc", "seq"), None),
        P(("doc", "seq"), None),
        P(("doc", "seq"), None),
        P(), P(), P(), P(), P(), P(),
    )
    out_specs = P(("doc", "seq"), None)
    return jax.shard_map(shards, mesh=mesh, in_specs=in_specs, out_specs=out_specs, check_vma=False)
```

```python
import functools
import jax
import jax.numpy as jnp
from jax import lax
from jax.experimental import pallas as pl
from jax.experimental.pallas import tpu as pltpu
from jax.sharding import PartitionSpec as P

HEADDIM = 64
STATE = 128
HEADS = 64
GROUP = 4
PARTS = 4
EXTRA = 16
MESH = pl.DeviceIdType.MESH


def shifted(value, axis, steps):
    count = lax.axis_size(axis)
    initial, last = (max(0, -steps), min(count, count - steps))
    return lax.ppermute(value, axis, [(source, source + steps) for source in range(initial, last)])


def convolve(conv_input, conv_weight, convolution_bias):
    tap_count = conv_weight.shape[0]
    row_count = conv_input.shape[0]
    earlier = shifted(conv_input[row_count - (tap_count - 1) :], "seq", 1)
    padded = jnp.concatenate([earlier, conv_input], axis=0).astype(jnp.float32)
    mixed = convolution_bias[None, :]
    for offset in range(tap_count):
        mixed = mixed + conv_weight[offset][None, :] * padded[offset : offset + row_count]
    return jax.nn.silu(mixed).astype(jnp.bfloat16)


def prefix_kernel(
    count, group, s_ref, f_ref, got, ein, eout, fsend, gsum,
    send_a, recv_a, send_c, recv_c, send_f, recv_f,
):
    rows = ein.shape[0]
    width = ein.shape[1]
    part = width // PARTS
    planes = count // group
    me = lax.axis_index("seq")
    mine = lax.rem(me, group)
    plane = me // group
    base = plane * group
    has_prev = plane > 0
    has_next = plane < planes - 1
    before = jnp.maximum(me - group, 0)
    after = jnp.minimum(me + group, count - 1)

    barrier = pltpu.get_barrier_semaphore()
    for step in range(1, group):
        other = base + lax.rem(mine + step, group)
        pl.semaphore_signal(barrier, inc=1, device_id={"seq": other}, device_id_type=MESH)

    @pl.when(has_prev)
    def _():
        pl.semaphore_signal(barrier, inc=1, device_id={"seq": before}, device_id_type=MESH)

    @pl.when(has_next)
    def _():
        pl.semaphore_signal(barrier, inc=1, device_id={"seq": after}, device_id_type=MESH)

    peers = group - 1 + jnp.minimum(plane, 1) + jnp.minimum(planes - 1 - plane, 1)
    pl.semaphore_wait(barrier, peers)

    def share(step, k):
        member = lax.rem(mine + step, group)
        return pltpu.make_async_remote_copy(
            src_ref=s_ref.at[:, pl.ds(pl.multiple_of(member * width + k * part, part), part)],
            dst_ref=got.at[step, :, pl.ds(k * part, part)],
            send_sem=send_a.at[step, k],
            recv_sem=recv_a.at[step, k],
            device_id={"seq": base + member},
            device_id_type=MESH,
        )

    def chain(k):
        columns = pl.ds(k * part, part)
        return pltpu.make_async_remote_copy(
            src_ref=eout.at[:, columns],
            dst_ref=ein.at[:, columns],
            send_sem=send_c.at[k],
            recv_sem=recv_c.at[k],
            device_id={"seq": after},
            device_id_type=MESH,
        )

    def back(step, k):
        member = lax.rem(mine + step, group)
        own = pl.ds(pl.multiple_of(mine * width + k * part, part), part)
        return pltpu.make_async_remote_copy(
            src_ref=fsend.at[step, :, pl.ds(k * part, part)],
            dst_ref=f_ref.at[:, own],
            send_sem=send_f.at[step, k],
            recv_sem=recv_f.at[step, k],
            device_id={"seq": base + member},
            device_id_type=MESH,
        )

    for k in range(PARTS):
        for step in range(1, group):
            share(step, k).start()
    got[0] = s_ref[:, pl.ds(pl.multiple_of(mine * width, width), width)]

    slots = [lax.rem(mine - i + group, group) for i in range(group)]
    for k in range(PARTS):
        columns = pl.ds(k * part, part)
        for step in range(1, group):
            share(step, k).wait_recv()
        running = jnp.zeros((rows, part), jnp.float32)
        level = jnp.zeros((1, part), jnp.float32)
        levels = [level]
        for i in range(group):
            tail = got[slots[i], rows : rows + EXTRA, columns].astype(jnp.float32)
            step_log = tail[0:1] + tail[1:2] + tail[2:3]
            running = jnp.exp(step_log) * running + got[slots[i], :rows, columns].astype(jnp.float32)
            gsum[i, :, columns] = running
            level = level + step_log
            levels.append(level)

        @pl.when(has_prev)
        def _():
            chain(k).wait_recv()

        @pl.when(jnp.logical_not(has_prev))
        def _():
            ein[:, columns] = jnp.zeros((rows, part), jnp.bfloat16)

        entering = ein[:, columns].astype(jnp.float32)

        @pl.when(has_next)
        def _():
            eout[:, columns] = (jnp.exp(levels[group]) * entering + gsum[group - 1, :, columns]).astype(jnp.bfloat16)
            chain(k).start()

        for j in range(group):
            if j == 0:
                value = entering
            else:
                value = jnp.exp(levels[j]) * entering + gsum[j - 1, :, columns]
            fsend[lax.rem(j - mine + group, group), :, columns] = value.astype(jnp.bfloat16)
        for step in range(1, group):
            back(step, k).start()
        own = pl.ds(pl.multiple_of(mine * width + k * part, part), part)
        f_ref[:, own] = fsend[0, :, columns]

    for k in range(PARTS):
        for step in range(1, group):
            share(step, k).wait_send()

        @pl.when(has_next)
        def _():
            chain(k).wait_send()

        for step in range(1, group):
            back(step, k).wait_send()
            source = lax.rem(mine - step + group, group)
            landed = pl.ds(pl.multiple_of(source * width + k * part, part), part)
            pltpu.make_async_remote_copy(
                src_ref=fsend.at[step, :, pl.ds(k * part, part)],
                dst_ref=f_ref.at[:, landed],
                send_sem=send_f.at[step, k],
                recv_sem=recv_f.at[step, k],
                device_id={"seq": base + lax.rem(mine + step, group)},
                device_id_type=MESH,
            ).wait_recv()


def entering_states(packed):
    count = lax.axis_size("seq")
    group = GROUP if count % GROUP == 0 else 1
    rows = packed.shape[0] - EXTRA
    width = packed.shape[1] // group
    return pl.pallas_call(
        functools.partial(prefix_kernel, count, group),
        out_shape=jax.ShapeDtypeStruct((rows, packed.shape[1]), jnp.bfloat16),
        in_specs=[pl.BlockSpec(memory_space=pltpu.VMEM)],
        out_specs=pl.BlockSpec(memory_space=pltpu.VMEM),
        scratch_shapes=[
            pltpu.VMEM((group, rows + EXTRA, width), jnp.bfloat16),
            pltpu.VMEM((rows, width), jnp.bfloat16),
            pltpu.VMEM((rows, width), jnp.bfloat16),
            pltpu.VMEM((group, rows, width), jnp.bfloat16),
            pltpu.VMEM((group, rows, width), jnp.float32),
            pltpu.SemaphoreType.DMA((group, PARTS)),
            pltpu.SemaphoreType.DMA((group, PARTS)),
            pltpu.SemaphoreType.DMA((PARTS,)),
            pltpu.SemaphoreType.DMA((PARTS,)),
            pltpu.SemaphoreType.DMA((group, PARTS)),
            pltpu.SemaphoreType.DMA((group, PARTS)),
        ],
        compiler_params=pltpu.CompilerParams(
            collective_id=0, has_side_effects=True, vmem_limit_bytes=32 * 1024 * 1024
        ),
    )(packed)


def split(value):
    high = value.astype(jnp.bfloat16)
    low = (value - high.astype(jnp.float32)).astype(jnp.bfloat16)
    return high, low


def mix_kernel(act, entering, gate, cols, rows_ref, steps, skip, gain, out, mixed):
    tokens = act.shape[0]
    inner = entering.shape[1]
    block = 8 * HEADDIM
    b_rows = act[:, inner : inner + STATE]
    c_rows = act[:, inner + STATE : inner + 2 * STATE]
    scores = lax.dot_general(c_rows, b_rows, (((1,), (1,)), ((), ())), preferred_element_type=jnp.float32)
    lower = lax.broadcasted_iota(jnp.int32, (tokens, tokens), 0) >= lax.broadcasted_iota(jnp.int32, (tokens, tokens), 1)
    scores = jnp.where(lower, scores, 0.0)
    c_wide = c_rows.astype(jnp.float32)
    first = lax.broadcasted_iota(jnp.int32, (tokens, 2 * HEADDIM), 1) < HEADDIM

    def body(g, carry):
        for pair in range(4):
            columns = pl.ds(pl.multiple_of(g * block + pair * 128, 128), 128)
            x = act[:, columns]
            stacked = jnp.concatenate([x, entering[:, columns]], axis=0)
            halves = []
            for half in range(2):
                h = pair * 2 + half
                col = cols[g, :, h : h + 1]
                row = rows_ref[g, h : h + 1, :]
                inside = jnp.exp(jnp.where(lower, col - row, -1e30)) * scores * steps[g, h : h + 1, :]
                whole = jnp.concatenate([inside, jnp.exp(col) * c_wide], axis=1)
                high, low = split(whole)
                halves.append(
                    jnp.dot(high, stacked, preferred_element_type=jnp.float32)
                    + jnp.dot(low, stacked, preferred_element_type=jnp.float32)
                )
            result = jnp.where(first, halves[0], halves[1]) + skip[:, columns] * x.astype(jnp.float32)
            mixed[:, columns] = result.astype(jnp.bfloat16)
        return carry

    lax.fori_loop(0, inner // block, body, 0)

    def norm(r, carry):
        take = pl.ds(pl.multiple_of(r * 16, 16), 16)
        z = gate[take, :].astype(jnp.float32)
        gated = mixed[take, :].astype(jnp.float32) * (z / (1.0 + jnp.exp(-z)))
        spread = jnp.mean(gated * gated, axis=-1, keepdims=True)
        out[take, :] = (gated * lax.rsqrt(spread + 1e-05) * gain[...]).astype(jnp.bfloat16)
        return carry

    lax.fori_loop(0, tokens // 16, norm, 0)


def shards(
    conv_input, gate_input, step_input, conv_weight, convolution_bias,
    step_bias, decay_log, skip_gain, norm_gain,
):
    highest = lax.Precision.HIGHEST
    inner = HEADS * HEADDIM
    tokens = conv_input.shape[0]
    activated = convolve(conv_input, conv_weight, convolution_bias)
    step_size = jax.nn.softplus(step_input.astype(jnp.float32) + step_bias[None, :])
    rate = -jnp.exp(decay_log)
    lower = (jnp.arange(tokens)[:, None] >= jnp.arange(tokens)[None, :]).astype(jnp.float32)
    within = jnp.dot(lower, step_size * rate[None, :], precision=highest)
    ends = within[-1]
    spread = (jnp.arange(inner)[None, :] // HEADDIM == jnp.arange(HEADS)[:, None]).astype(jnp.bfloat16)
    tail = jnp.exp(ends[None, :] - within) * step_size
    top = lax.reduce_precision(tail, 8, 7)
    tail = jnp.dot(
        jnp.concatenate([top, tail - top], axis=1).astype(jnp.bfloat16),
        jnp.concatenate([spread, spread], axis=0),
        preferred_element_type=jnp.float32,
    )
    weighted = (tail * activated[:, :inner].astype(jnp.float32)).astype(jnp.bfloat16)
    state = lax.dot_general(
        activated[:, inner : inner + STATE], weighted, (((0,), (0,)), ((), ())),
        preferred_element_type=jnp.float32,
    ).astype(jnp.bfloat16)
    high = lax.reduce_precision(ends, 8, 7)
    middle = lax.reduce_precision(ends - high, 8, 7)
    low = lax.reduce_precision(ends - high - middle, 8, 7)
    logs = jnp.stack([high, middle, low] + [jnp.zeros_like(low)] * (EXTRA - 3)).astype(jnp.bfloat16)
    logs = jnp.dot(logs, spread, preferred_element_type=jnp.float32).astype(jnp.bfloat16)
    packed = jnp.concatenate([state, logs], axis=0)
    entering = entering_states(packed)
    groups = HEADS // 8
    cols = jnp.transpose(within.reshape(tokens, groups, 8), (1, 0, 2))
    rows = jnp.transpose(within).reshape(groups, 8, tokens)
    steps = jnp.transpose(step_size).reshape(groups, 8, tokens)
    skip = jnp.repeat(skip_gain, HEADDIM)[None, :]
    return pl.pallas_call(
        mix_kernel,
        out_shape=jax.ShapeDtypeStruct((tokens, inner), jnp.bfloat16),
        in_specs=[pl.BlockSpec(memory_space=pltpu.VMEM)] * 8,
        out_specs=pl.BlockSpec(memory_space=pltpu.VMEM),
        scratch_shapes=[pltpu.VMEM((tokens, inner), jnp.bfloat16)],
        compiler_params=pltpu.CompilerParams(vmem_limit_bytes=32 * 1024 * 1024),
    )(activated, entering, gate_input, cols, rows, steps, skip, norm_gain[None, :])


def solution(mesh):
    in_specs = (
        P(("doc", "seq"), None),
        P(("doc", "seq"), None),
        P(("doc", "seq"), None),
        P(), P(), P(), P(), P(), P(),
    )
    out_specs = P(("doc", "seq"), None)
    return jax.shard_map(shards, mesh=mesh, in_specs=in_specs, out_specs=out_specs, check_vma=False)
```

```python
import functools
import jax
import jax.numpy as jnp
from jax import lax
from jax.experimental import pallas as pl
from jax.experimental.pallas import tpu as pltpu
from jax.sharding import PartitionSpec as P

HEADDIM = 64
STATE = 128
HEADS = 64
GROUP = 4
PARTS = 4
EXTRA = 16
MESH = pl.DeviceIdType.MESH


def shifted(value, axis, steps):
    count = lax.axis_size(axis)
    initial, last = (max(0, -steps), min(count, count - steps))
    return lax.ppermute(value, axis, [(source, source + steps) for source in range(initial, last)])


def convolve(conv_input, conv_weight, convolution_bias):
    tap_count = conv_weight.shape[0]
    row_count = conv_input.shape[0]
    earlier = shifted(conv_input[row_count - (tap_count - 1) :], "seq", 1)
    padded = jnp.concatenate([earlier, conv_input], axis=0).astype(jnp.float32)
    mixed = convolution_bias[None, :]
    for offset in range(tap_count):
        mixed = mixed + conv_weight[offset][None, :] * padded[offset : offset + row_count]
    return jax.nn.silu(mixed).astype(jnp.bfloat16)


def split(value):
    high = value.astype(jnp.bfloat16)
    low = (value - high.astype(jnp.float32)).astype(jnp.bfloat16)
    return high, low


def prefix_kernel(
    count, group, s_ref, act, gate, cols, rows_ref, steps, skip, gain,
    out, f_ref, mixed, got, ein, eout, fsend, gsum,
    send_a, recv_a, send_c, recv_c, send_f, recv_f,
):
    rows = ein.shape[0]
    width = ein.shape[1]
    part = width // PARTS
    planes = count // group
    me = lax.axis_index("seq")
    mine = lax.rem(me, group)
    plane = me // group
    base = plane * group
    has_prev = plane > 0
    has_next = plane < planes - 1
    before = jnp.maximum(me - group, 0)
    after = jnp.minimum(me + group, count - 1)

    barrier = pltpu.get_barrier_semaphore()
    for step in range(1, group):
        other = base + lax.rem(mine + step, group)
        pl.semaphore_signal(barrier, inc=1, device_id={"seq": other}, device_id_type=MESH)

    @pl.when(has_prev)
    def _():
        pl.semaphore_signal(barrier, inc=1, device_id={"seq": before}, device_id_type=MESH)

    @pl.when(has_next)
    def _():
        pl.semaphore_signal(barrier, inc=1, device_id={"seq": after}, device_id_type=MESH)

    peers = group - 1 + jnp.minimum(plane, 1) + jnp.minimum(planes - 1 - plane, 1)
    pl.semaphore_wait(barrier, peers)

    def share(step, k):
        member = lax.rem(mine + step, group)
        return pltpu.make_async_remote_copy(
            src_ref=s_ref.at[:, pl.ds(pl.multiple_of(member * width + k * part, part), part)],
            dst_ref=got.at[step, :, pl.ds(k * part, part)],
            send_sem=send_a.at[step, k],
            recv_sem=recv_a.at[step, k],
            device_id={"seq": base + member},
            device_id_type=MESH,
        )

    def chain(k):
        columns = pl.ds(k * part, part)
        return pltpu.make_async_remote_copy(
            src_ref=eout.at[:, columns],
            dst_ref=ein.at[:, columns],
            send_sem=send_c.at[k],
            recv_sem=recv_c.at[k],
            device_id={"seq": after},
            device_id_type=MESH,
        )

    def back(step, k):
        member = lax.rem(mine + step, group)
        own = pl.ds(pl.multiple_of(mine * width + k * part, part), part)
        return pltpu.make_async_remote_copy(
            src_ref=fsend.at[step, :, pl.ds(k * part, part)],
            dst_ref=f_ref.at[:, own],
            send_sem=send_f.at[step, k],
            recv_sem=recv_f.at[step, k],
            device_id={"seq": base + member},
            device_id_type=MESH,
        )

    for k in range(PARTS):
        for step in range(1, group):
            share(step, k).start()
    got[0] = s_ref[:, pl.ds(pl.multiple_of(mine * width, width), width)]

    tokens = act.shape[0]
    inner = f_ref.shape[1]
    block = 8 * HEADDIM
    blocks = inner // block
    b_rows = act[:, inner : inner + STATE]
    c_rows = act[:, inner + STATE : inner + 2 * STATE]
    scores = lax.dot_general(c_rows, b_rows, (((1,), (1,)), ((), ())), preferred_element_type=jnp.float32)
    lower = lax.broadcasted_iota(jnp.int32, (tokens, tokens), 0) >= lax.broadcasted_iota(jnp.int32, (tokens, tokens), 1)
    scores = jnp.where(lower, scores, 0.0)
    first = lax.broadcasted_iota(jnp.int32, (tokens, 2 * HEADDIM), 1) < HEADDIM

    def inside_block(g, carry):
        for pair in range(4):
            columns = pl.ds(pl.multiple_of(g * block + pair * 128, 128), 128)
            x = act[:, columns]
            stacked = jnp.concatenate([x, x], axis=0)
            halves = []
            for half in range(2):
                h = pair * 2 + half
                col = cols[g, :, h : h + 1]
                row = rows_ref[g, h : h + 1, :]
                inside = jnp.exp(jnp.where(lower, col - row, -1e30)) * scores * steps[g, h : h + 1, :]
                halves.append(
                    jnp.dot(
                        jnp.concatenate(split(inside), axis=1), stacked,
                        preferred_element_type=jnp.float32,
                    )
                )
            mixed[:, columns] = jnp.where(first, halves[0], halves[1]) + skip[:, columns] * x.astype(jnp.float32)
        return carry

    ahead = (blocks * plane) // max(planes - 1, 1)
    lax.fori_loop(0, ahead, inside_block, 0)

    slots = [lax.rem(mine - i + group, group) for i in range(group)]
    for k in range(PARTS):
        columns = pl.ds(k * part, part)
        for step in range(1, group):
            share(step, k).wait_recv()
        running = jnp.zeros((rows, part), jnp.float32)
        level = jnp.zeros((1, part), jnp.float32)
        levels = [level]
        for i in range(group):
            tail = got[slots[i], rows : rows + EXTRA, columns].astype(jnp.float32)
            step_log = tail[0:1] + tail[1:2] + tail[2:3]
            running = jnp.exp(step_log) * running + got[slots[i], :rows, columns].astype(jnp.float32)
            gsum[i, :, columns] = running
            level = level + step_log
            levels.append(level)

        @pl.when(has_prev)
        def _():
            chain(k).wait_recv()

        @pl.when(jnp.logical_not(has_prev))
        def _():
            ein[:, columns] = jnp.zeros((rows, part), jnp.bfloat16)

        entering = ein[:, columns].astype(jnp.float32)

        @pl.when(has_next)
        def _():
            eout[:, columns] = (jnp.exp(levels[group]) * entering + gsum[group - 1, :, columns]).astype(jnp.bfloat16)
            chain(k).start()

        for j in range(group):
            if j == 0:
                value = entering
            else:
                value = jnp.exp(levels[j]) * entering + gsum[j - 1, :, columns]
            fsend[lax.rem(j - mine + group, group), :, columns] = value.astype(jnp.bfloat16)
        for step in range(1, group):
            back(step, k).start()
        own = pl.ds(pl.multiple_of(mine * width + k * part, part), part)
        f_ref[:, own] = fsend[0, :, columns]

    lax.fori_loop(ahead, blocks, inside_block, 0)

    for k in range(PARTS):
        for step in range(1, group):
            share(step, k).wait_send()

        @pl.when(has_next)
        def _():
            chain(k).wait_send()

        for step in range(1, group):
            back(step, k).wait_send()
            source = lax.rem(mine - step + group, group)
            landed = pl.ds(pl.multiple_of(source * width + k * part, part), part)
            pltpu.make_async_remote_copy(
                src_ref=fsend.at[step, :, pl.ds(k * part, part)],
                dst_ref=f_ref.at[:, landed],
                send_sem=send_f.at[step, k],
                recv_sem=recv_f.at[step, k],
                device_id={"seq": base + lax.rem(mine + step, group)},
                device_id_type=MESH,
            ).wait_recv()

    def outside_block(g, carry):
        wide = pl.ds(pl.multiple_of(g * block, block), block)
        outer = jnp.dot(c_rows, f_ref[:, wide], preferred_element_type=jnp.float32)
        for pair in range(4):
            columns = pl.ds(pl.multiple_of(g * block + pair * 128, 128), 128)
            level = jnp.where(first, cols[g, :, 2 * pair : 2 * pair + 1], cols[g, :, 2 * pair + 1 : 2 * pair + 2])
            mixed[:, columns] += jnp.exp(level) * outer[:, pair * 128 : pair * 128 + 128]
        return carry

    lax.fori_loop(0, blocks, outside_block, 0)

    def norm(r, carry):
        take = pl.ds(pl.multiple_of(r * 16, 16), 16)
        z = gate[take, :].astype(jnp.float32)
        result = mixed[take, :].astype(jnp.bfloat16).astype(jnp.float32)
        gated = result * (z / (1.0 + jnp.exp(-z)))
        spread = jnp.mean(gated * gated, axis=-1, keepdims=True)
        out[take, :] = (gated * lax.rsqrt(spread + 1e-05) * gain[...]).astype(jnp.bfloat16)
        return carry

    lax.fori_loop(0, tokens // 16, norm, 0)


def mixer(packed, activated, *others):
    count = lax.axis_size("seq")
    group = GROUP if count % GROUP == 0 else 1
    rows = packed.shape[0] - EXTRA
    width = packed.shape[1] // group
    return pl.pallas_call(
        functools.partial(prefix_kernel, count, group),
        out_shape=jax.ShapeDtypeStruct((activated.shape[0], packed.shape[1]), jnp.bfloat16),
        in_specs=[pl.BlockSpec(memory_space=pltpu.VMEM)] * (2 + len(others)),
        out_specs=pl.BlockSpec(memory_space=pltpu.VMEM),
        scratch_shapes=[
            pltpu.VMEM((rows, packed.shape[1]), jnp.bfloat16),
            pltpu.VMEM((activated.shape[0], packed.shape[1]), jnp.float32),
            pltpu.VMEM((group, rows + EXTRA, width), jnp.bfloat16),
            pltpu.VMEM((rows, width), jnp.bfloat16),
            pltpu.VMEM((rows, width), jnp.bfloat16),
            pltpu.VMEM((group, rows, width), jnp.bfloat16),
            pltpu.VMEM((group, rows, width), jnp.float32),
            pltpu.SemaphoreType.DMA((group, PARTS)),
            pltpu.SemaphoreType.DMA((group, PARTS)),
            pltpu.SemaphoreType.DMA((PARTS,)),
            pltpu.SemaphoreType.DMA((PARTS,)),
            pltpu.SemaphoreType.DMA((group, PARTS)),
            pltpu.SemaphoreType.DMA((group, PARTS)),
        ],
        compiler_params=pltpu.CompilerParams(
            collective_id=0, has_side_effects=True, vmem_limit_bytes=32 * 1024 * 1024
        ),
    )(packed, activated, *others)


def shards(
    conv_input, gate_input, step_input, conv_weight, convolution_bias,
    step_bias, decay_log, skip_gain, norm_gain,
):
    highest = lax.Precision.HIGHEST
    inner = HEADS * HEADDIM
    tokens = conv_input.shape[0]
    activated = convolve(conv_input, conv_weight, convolution_bias)
    step_size = jax.nn.softplus(step_input.astype(jnp.float32) + step_bias[None, :])
    rate = -jnp.exp(decay_log)
    lower = (jnp.arange(tokens)[:, None] >= jnp.arange(tokens)[None, :]).astype(jnp.float32)
    within = jnp.dot(lower, step_size * rate[None, :], precision=highest)
    ends = within[-1]
    spread = (jnp.arange(inner)[None, :] // HEADDIM == jnp.arange(HEADS)[:, None]).astype(jnp.bfloat16)
    tail = jnp.exp(ends[None, :] - within) * step_size
    top = lax.reduce_precision(tail, 8, 7)
    tail = jnp.dot(
        jnp.concatenate([top, tail - top], axis=1).astype(jnp.bfloat16),
        jnp.concatenate([spread, spread], axis=0),
        preferred_element_type=jnp.float32,
    )
    weighted = (tail * activated[:, :inner].astype(jnp.float32)).astype(jnp.bfloat16)
    state = lax.dot_general(
        activated[:, inner : inner + STATE], weighted, (((0,), (0,)), ((), ())),
        preferred_element_type=jnp.float32,
    ).astype(jnp.bfloat16)
    high = lax.reduce_precision(ends, 8, 7)
    middle = lax.reduce_precision(ends - high, 8, 7)
    low = lax.reduce_precision(ends - high - middle, 8, 7)
    logs = jnp.stack([high, middle, low] + [jnp.zeros_like(low)] * (EXTRA - 3)).astype(jnp.bfloat16)
    logs = jnp.dot(logs, spread, preferred_element_type=jnp.float32).astype(jnp.bfloat16)
    packed = jnp.concatenate([state, logs], axis=0)
    groups = HEADS // 8
    cols = jnp.transpose(within.reshape(tokens, groups, 8), (1, 0, 2))
    rows = jnp.transpose(within).reshape(groups, 8, tokens)
    steps = jnp.transpose(step_size).reshape(groups, 8, tokens)
    skip = jnp.repeat(skip_gain, HEADDIM)[None, :]
    return mixer(packed, activated, gate_input, cols, rows, steps, skip, norm_gain[None, :])


def solution(mesh):
    in_specs = (
        P(("doc", "seq"), None),
        P(("doc", "seq"), None),
        P(("doc", "seq"), None),
        P(), P(), P(), P(), P(), P(),
    )
    out_specs = P(("doc", "seq"), None)
    return jax.shard_map(shards, mesh=mesh, in_specs=in_specs, out_specs=out_specs, check_vma=False)
```

```python
import functools
import jax
import jax.numpy as jnp
from jax import lax
from jax.experimental import pallas as pl
from jax.experimental.pallas import tpu as pltpu
from jax.sharding import PartitionSpec as P

HEADDIM = 64
STATE = 128
HEADS = 64
GROUP = 4
PARTS = 4
EXTRA = 16
MESH = pl.DeviceIdType.MESH


def shifted(value, axis, steps):
    count = lax.axis_size(axis)
    initial, last = (max(0, -steps), min(count, count - steps))
    return lax.ppermute(value, axis, [(source, source + steps) for source in range(initial, last)])


def convolve(conv_input, conv_weight, convolution_bias):
    tap_count = conv_weight.shape[0]
    row_count = conv_input.shape[0]
    earlier = shifted(conv_input[row_count - (tap_count - 1) :], "seq", 1)
    padded = jnp.concatenate([earlier, conv_input], axis=0).astype(jnp.float32)
    mixed = convolution_bias[None, :]
    for offset in range(tap_count):
        mixed = mixed + conv_weight[offset][None, :] * padded[offset : offset + row_count]
    return jax.nn.silu(mixed).astype(jnp.bfloat16)


def split(value):
    high = value.astype(jnp.bfloat16)
    low = (value - high.astype(jnp.float32)).astype(jnp.bfloat16)
    return high, low


def prefix_kernel(
    count, group, tails, logs, act, gate, cols, rows_ref, steps, skip, gain,
    out, s_ref, f_ref, mixed, squares, got, ein, eout, fsend, gsum,
    send_a, recv_a, send_c, recv_c, send_f, recv_f,
):
    rows = ein.shape[0]
    width = ein.shape[1]
    part = width // PARTS
    planes = count // group
    me = lax.axis_index("seq")
    mine = lax.rem(me, group)
    plane = me // group
    base = plane * group
    has_prev = plane > 0
    has_next = plane < planes - 1
    before = jnp.maximum(me - group, 0)
    after = jnp.minimum(me + group, count - 1)

    barrier = pltpu.get_barrier_semaphore()
    for step in range(1, group):
        other = base + lax.rem(mine + step, group)
        pl.semaphore_signal(barrier, inc=1, device_id={"seq": other}, device_id_type=MESH)

    @pl.when(has_prev)
    def _():
        pl.semaphore_signal(barrier, inc=1, device_id={"seq": before}, device_id_type=MESH)

    @pl.when(has_next)
    def _():
        pl.semaphore_signal(barrier, inc=1, device_id={"seq": after}, device_id_type=MESH)

    peers = group - 1 + jnp.minimum(plane, 1) + jnp.minimum(planes - 1 - plane, 1)
    pl.semaphore_wait(barrier, peers)

    def share(step, k):
        member = lax.rem(mine + step, group)
        return pltpu.make_async_remote_copy(
            src_ref=s_ref.at[:, pl.ds(pl.multiple_of(member * width + k * part, part), part)],
            dst_ref=got.at[step, :, pl.ds(k * part, part)],
            send_sem=send_a.at[step, k],
            recv_sem=recv_a.at[step, k],
            device_id={"seq": base + member},
            device_id_type=MESH,
        )

    def chain(k):
        columns = pl.ds(k * part, part)
        return pltpu.make_async_remote_copy(
            src_ref=eout.at[:, columns],
            dst_ref=ein.at[:, columns],
            send_sem=send_c.at[k],
            recv_sem=recv_c.at[k],
            device_id={"seq": after},
            device_id_type=MESH,
        )

    def back(step, k):
        member = lax.rem(mine + step, group)
        own = pl.ds(pl.multiple_of(mine * width + k * part, part), part)
        return pltpu.make_async_remote_copy(
            src_ref=fsend.at[step, :, pl.ds(k * part, part)],
            dst_ref=f_ref.at[:, own],
            send_sem=send_f.at[step, k],
            recv_sem=recv_f.at[step, k],
            device_id={"seq": base + member},
            device_id_type=MESH,
        )

    inner = f_ref.shape[1]
    b_rows = act[:, inner : inner + STATE]
    turned = jnp.transpose(b_rows.astype(jnp.float32)).astype(jnp.bfloat16)
    factors = tails[...]
    lane = lax.broadcasted_iota(jnp.int32, (2 * HEADS, part), 1)
    head = lax.rem(lax.broadcasted_iota(jnp.int32, (2 * HEADS, part), 0), HEADS)

    def local_state(start):
        low = head * HEADDIM - start
        spread = jnp.where((lane >= low) & (lane < low + HEADDIM), 1.0, 0.0).astype(jnp.bfloat16)
        tail = jnp.dot(factors, spread, preferred_element_type=jnp.float32)
        weighted = (tail * act[:, pl.ds(start, part)].astype(jnp.float32)).astype(jnp.bfloat16)
        state = jnp.dot(turned, weighted, preferred_element_type=jnp.float32).astype(jnp.bfloat16)
        return state, jnp.dot(logs[...], spread, preferred_element_type=jnp.float32).astype(jnp.bfloat16)

    for k in range(PARTS):
        for step in range(1, group):
            member = lax.rem(mine + step, group)
            start = pl.multiple_of(member * width + k * part, part)
            state, marks = local_state(start)
            s_ref[:rows, pl.ds(start, part)] = state
            s_ref[rows:, pl.ds(start, part)] = marks
            share(step, k).start()
    for k in range(PARTS):
        state, marks = local_state(pl.multiple_of(mine * width + k * part, part))
        got[0, :rows, pl.ds(k * part, part)] = state
        got[0, rows:, pl.ds(k * part, part)] = marks

    tokens = act.shape[0]
    block = 8 * HEADDIM
    blocks = inner // block
    c_rows = act[:, inner + STATE : inner + 2 * STATE]
    scores = lax.dot_general(c_rows, b_rows, (((1,), (1,)), ((), ())), preferred_element_type=jnp.float32)
    lower = lax.broadcasted_iota(jnp.int32, (tokens, tokens), 0) >= lax.broadcasted_iota(jnp.int32, (tokens, tokens), 1)
    scores = jnp.where(lower, scores, 0.0)
    first = lax.broadcasted_iota(jnp.int32, (tokens, 2 * HEADDIM), 1) < HEADDIM

    def inside_block(g, carry):
        for pair in range(4):
            columns = pl.ds(pl.multiple_of(g * block + pair * 128, 128), 128)
            x = act[:, columns]
            stacked = jnp.concatenate([x, x], axis=0)
            halves = []
            for half in range(2):
                h = pair * 2 + half
                col = cols[g, :, h : h + 1]
                row = rows_ref[g, h : h + 1, :]
                inside = jnp.exp(jnp.where(lower, col - row, -1e30)) * scores * steps[g, h : h + 1, :]
                halves.append(
                    jnp.dot(
                        jnp.concatenate(split(inside), axis=1), stacked,
                        preferred_element_type=jnp.float32,
                    )
                )
            mixed[:, columns] = jnp.where(first, halves[0], halves[1]) + skip[:, columns] * x.astype(jnp.float32)
        return carry

    ahead = (blocks * plane) // max(planes - 1, 1)
    lax.fori_loop(0, ahead, inside_block, 0)

    slots = [lax.rem(mine - i + group, group) for i in range(group)]
    for k in range(PARTS):
        columns = pl.ds(k * part, part)
        for step in range(1, group):
            share(step, k).wait_recv()
        running = jnp.zeros((rows, part), jnp.float32)
        level = jnp.zeros((1, part), jnp.float32)
        levels = [level]
        for i in range(group):
            tail = got[slots[i], rows : rows + EXTRA, columns].astype(jnp.float32)
            step_log = tail[0:1] + tail[1:2] + tail[2:3]
            running = jnp.exp(step_log) * running + got[slots[i], :rows, columns].astype(jnp.float32)
            gsum[i, :, columns] = running
            level = level + step_log
            levels.append(level)

        @pl.when(has_prev)
        def _():
            chain(k).wait_recv()

        @pl.when(jnp.logical_not(has_prev))
        def _():
            ein[:, columns] = jnp.zeros((rows, part), jnp.bfloat16)

        entering = ein[:, columns].astype(jnp.float32)

        @pl.when(has_next)
        def _():
            eout[:, columns] = (jnp.exp(levels[group]) * entering + gsum[group - 1, :, columns]).astype(jnp.bfloat16)
            chain(k).start()

        for j in range(group):
            if j == 0:
                value = entering
            else:
                value = jnp.exp(levels[j]) * entering + gsum[j - 1, :, columns]
            fsend[lax.rem(j - mine + group, group), :, columns] = value.astype(jnp.bfloat16)
        for step in range(1, group):
            back(step, k).start()
        own = pl.ds(pl.multiple_of(mine * width + k * part, part), part)
        f_ref[:, own] = fsend[0, :, columns]

    lax.fori_loop(ahead, blocks, inside_block, 0)

    def outside(source, k):
        where = pl.multiple_of(source * width + k * part, part)
        outer = jnp.dot(c_rows, f_ref[:, pl.ds(where, part)], preferred_element_type=jnp.float32)
        for pair in range(part // 128):
            offset = (k * part) // HEADDIM + 2 * pair
            g, h = source * (width // block) + offset // 8, offset % 8
            columns = pl.ds(pl.multiple_of(where + pair * 128, 128), 128)
            level = jnp.where(first, cols[g, :, h : h + 1], cols[g, :, h + 1 : h + 2])
            total = mixed[:, columns] + jnp.exp(level) * outer[:, pair * 128 : pair * 128 + 128]
            z = gate[:, columns].astype(jnp.float32)
            gated = total.astype(jnp.bfloat16).astype(jnp.float32) * (z / (1.0 + jnp.exp(-z)))
            mixed[:, columns] = gated
            squares[...] += gated * gated

    squares[...] = jnp.zeros_like(squares)
    for k in range(PARTS):
        outside(mine, k)
        for step in range(1, group):
            source = lax.rem(mine - step + group, group)
            landed = pl.ds(pl.multiple_of(source * width + k * part, part), part)
            pltpu.make_async_remote_copy(
                src_ref=fsend.at[step, :, pl.ds(k * part, part)],
                dst_ref=f_ref.at[:, landed],
                send_sem=send_f.at[step, k],
                recv_sem=recv_f.at[step, k],
                device_id={"seq": base + lax.rem(mine + step, group)},
                device_id_type=MESH,
            ).wait_recv()
            outside(source, k)

    def norm(r, carry):
        take = pl.ds(pl.multiple_of(r * 16, 16), 16)
        mean = jnp.sum(squares[take, :], axis=-1, keepdims=True) * (1.0 / inner)
        out[take, :] = (mixed[take, :] * lax.rsqrt(mean + 1e-05) * gain[...]).astype(jnp.bfloat16)
        return carry

    lax.fori_loop(0, tokens // 16, norm, 0)

    for k in range(PARTS):
        for step in range(1, group):
            share(step, k).wait_send()
            back(step, k).wait_send()

        @pl.when(has_next)
        def _():
            chain(k).wait_send()


def mixer(tails, logs, activated, *others):
    count = lax.axis_size("seq")
    group = GROUP if count % GROUP == 0 else 1
    rows = STATE
    inner = HEADS * HEADDIM
    width = inner // group
    tokens = activated.shape[0]
    return pl.pallas_call(
        functools.partial(prefix_kernel, count, group),
        out_shape=jax.ShapeDtypeStruct((tokens, inner), jnp.bfloat16),
        in_specs=[pl.BlockSpec(memory_space=pltpu.VMEM)] * (3 + len(others)),
        out_specs=pl.BlockSpec(memory_space=pltpu.VMEM),
        scratch_shapes=[
            pltpu.VMEM((rows + EXTRA, inner), jnp.bfloat16),
            pltpu.VMEM((rows, inner), jnp.bfloat16),
            pltpu.VMEM((tokens, inner), jnp.float32),
            pltpu.VMEM((tokens, 128), jnp.float32),
            pltpu.VMEM((group, rows + EXTRA, width), jnp.bfloat16),
            pltpu.VMEM((rows, width), jnp.bfloat16),
            pltpu.VMEM((rows, width), jnp.bfloat16),
            pltpu.VMEM((group, rows, width), jnp.bfloat16),
            pltpu.VMEM((group, rows, width), jnp.float32),
            pltpu.SemaphoreType.DMA((group, PARTS)),
            pltpu.SemaphoreType.DMA((group, PARTS)),
            pltpu.SemaphoreType.DMA((PARTS,)),
            pltpu.SemaphoreType.DMA((PARTS,)),
            pltpu.SemaphoreType.DMA((group, PARTS)),
            pltpu.SemaphoreType.DMA((group, PARTS)),
        ],
        compiler_params=pltpu.CompilerParams(
            collective_id=0, has_side_effects=True, vmem_limit_bytes=32 * 1024 * 1024
        ),
    )(tails, logs, activated, *others)


def shards(
    conv_input, gate_input, step_input, conv_weight, convolution_bias,
    step_bias, decay_log, skip_gain, norm_gain,
):
    highest = lax.Precision.HIGHEST
    inner = HEADS * HEADDIM
    tokens = conv_input.shape[0]
    activated = convolve(conv_input, conv_weight, convolution_bias)
    step_size = jax.nn.softplus(step_input.astype(jnp.float32) + step_bias[None, :])
    rate = -jnp.exp(decay_log)
    lower = (jnp.arange(tokens)[:, None] >= jnp.arange(tokens)[None, :]).astype(jnp.float32)
    within = jnp.dot(lower, step_size * rate[None, :], precision=highest)
    ends = within[-1]
    tail = jnp.exp(ends[None, :] - within) * step_size
    top = lax.reduce_precision(tail, 8, 7)
    tails = jnp.concatenate([top, tail - top], axis=1).astype(jnp.bfloat16)
    high = lax.reduce_precision(ends, 8, 7)
    middle = lax.reduce_precision(ends - high, 8, 7)
    low = lax.reduce_precision(ends - high - middle, 8, 7)
    logs = jnp.stack([high, middle, low] + [jnp.zeros_like(low)] * (EXTRA - 3)).astype(jnp.bfloat16)
    logs = jnp.concatenate([logs, jnp.zeros_like(logs)], axis=1)
    groups = HEADS // 8
    cols = jnp.transpose(within.reshape(tokens, groups, 8), (1, 0, 2))
    rows = jnp.transpose(within).reshape(groups, 8, tokens)
    steps = jnp.transpose(step_size).reshape(groups, 8, tokens)
    skip = jnp.repeat(skip_gain, HEADDIM)[None, :]
    return mixer(tails, logs, activated, gate_input, cols, rows, steps, skip, norm_gain[None, :])


def solution(mesh):
    in_specs = (
        P(("doc", "seq"), None),
        P(("doc", "seq"), None),
        P(("doc", "seq"), None),
        P(), P(), P(), P(), P(), P(),
    )
    out_specs = P(("doc", "seq"), None)
    return jax.shard_map(shards, mesh=mesh, in_specs=in_specs, out_specs=out_specs, check_vma=False)
```

```python
import functools
import jax
import jax.numpy as jnp
from jax import lax
from jax.experimental import pallas as pl
from jax.experimental.pallas import tpu as pltpu
from jax.sharding import PartitionSpec as P

HEADDIM = 64
STATE = 128
HEADS = 64
GROUP = 4
PARTS = 4
EXTRA = 16
MESH = pl.DeviceIdType.MESH


def split(value):
    high = value.astype(jnp.bfloat16)
    low = (value - high.astype(jnp.float32)).astype(jnp.bfloat16)
    return high, low


def prefix_kernel(
    count, group, tails, logs, conv, weight, bias, gate, cols, rows_ref, steps, gain,
    out, act, padded, halo, skip, s_ref, f_ref, mixed, squares, got, ein, eout, fsend, gsum,
    send_h, recv_h, send_a, recv_a, send_c, recv_c, send_f, recv_f,
):
    rows = ein.shape[0]
    width = ein.shape[1]
    part = width // PARTS
    planes = count // group
    me = lax.axis_index("seq")
    mine = lax.rem(me, group)
    plane = me // group
    base = plane * group
    has_prev = plane > 0
    has_next = plane < planes - 1
    before = jnp.maximum(me - group, 0)
    after = jnp.minimum(me + group, count - 1)

    barrier = pltpu.get_barrier_semaphore()
    for step in range(1, group):
        other = base + lax.rem(mine + step, group)
        pl.semaphore_signal(barrier, inc=1, device_id={"seq": other}, device_id_type=MESH)

    @pl.when(has_prev)
    def _():
        pl.semaphore_signal(barrier, inc=1, device_id={"seq": before}, device_id_type=MESH)

    @pl.when(has_next)
    def _():
        pl.semaphore_signal(barrier, inc=1, device_id={"seq": after}, device_id_type=MESH)

    is_last = mine // max(group - 1, 1)
    is_first = 1 - jnp.minimum(mine, 1)

    @pl.when(has_prev & (is_first == 1))
    def _():
        pl.semaphore_signal(barrier, inc=1, device_id={"seq": jnp.maximum(me - 1, 0)}, device_id_type=MESH)

    @pl.when(has_next & (is_last == 1))
    def _():
        pl.semaphore_signal(barrier, inc=1, device_id={"seq": jnp.minimum(me + 1, count - 1)}, device_id_type=MESH)

    peers = group - 1 + jnp.minimum(plane, 1) * (1 + is_first) + jnp.minimum(planes - 1 - plane, 1) * (1 + is_last)
    pl.semaphore_wait(barrier, peers)

    def share(step, k):
        member = lax.rem(mine + step, group)
        return pltpu.make_async_remote_copy(
            src_ref=s_ref.at[:, pl.ds(pl.multiple_of(member * width + k * part, part), part)],
            dst_ref=got.at[step, :, pl.ds(k * part, part)],
            send_sem=send_a.at[step, k],
            recv_sem=recv_a.at[step, k],
            device_id={"seq": base + member},
            device_id_type=MESH,
        )

    def chain(k):
        columns = pl.ds(k * part, part)
        return pltpu.make_async_remote_copy(
            src_ref=eout.at[:, columns],
            dst_ref=ein.at[:, columns],
            send_sem=send_c.at[k],
            recv_sem=recv_c.at[k],
            device_id={"seq": after},
            device_id_type=MESH,
        )

    def back(step, k):
        member = lax.rem(mine + step, group)
        own = pl.ds(pl.multiple_of(mine * width + k * part, part), part)
        return pltpu.make_async_remote_copy(
            src_ref=fsend.at[step, :, pl.ds(k * part, part)],
            dst_ref=f_ref.at[:, own],
            send_sem=send_f.at[step, k],
            recv_sem=recv_f.at[step, k],
            device_id={"seq": base + member},
            device_id_type=MESH,
        )

    inner = f_ref.shape[1]
    tokens = conv.shape[0]
    taps = weight.shape[0]
    hand_on = pltpu.make_async_remote_copy(
        src_ref=conv.at[pl.ds(tokens - EXTRA, EXTRA)],
        dst_ref=halo,
        send_sem=send_h,
        recv_sem=recv_h,
        device_id={"seq": jnp.minimum(me + 1, count - 1)},
        device_id_type=MESH,
    )

    @pl.when(me < count - 1)
    def _():
        hand_on.start()

    padded[8:, :] = conv[...].astype(jnp.float32)

    @pl.when(me == 0)
    def _():
        halo[...] = jnp.zeros_like(halo)

    @pl.when(me > 0)
    def _():
        hand_on.wait_recv()

    padded[:8, :] = halo[...].astype(jnp.float32)[8:]

    def activate(start, size):
        where = pl.ds(start, size)
        value = bias[:, where]
        for tap in range(taps):
            value = value + weight[tap : tap + 1, where] * padded[pl.ds(9 - taps + tap, tokens), where]
        act[:, where] = (value / (1.0 + jnp.exp(-value))).astype(jnp.bfloat16)

    activate(inner, 2 * STATE)
    b_rows = act[:, inner : inner + STATE]
    turned = jnp.transpose(b_rows.astype(jnp.float32)).astype(jnp.bfloat16)
    factors = tails[...]
    lane = lax.broadcasted_iota(jnp.int32, (2 * HEADS, part), 1)
    head = lax.rem(lax.broadcasted_iota(jnp.int32, (2 * HEADS, part), 0), HEADS)

    def local_state(start):
        activate(start, part)
        low = head * HEADDIM - start
        spread = jnp.where((lane >= low) & (lane < low + HEADDIM), 1.0, 0.0).astype(jnp.bfloat16)
        tail = jnp.dot(factors, spread, preferred_element_type=jnp.float32)
        weighted = (tail * act[:, pl.ds(start, part)].astype(jnp.float32)).astype(jnp.bfloat16)
        state = jnp.dot(turned, weighted, preferred_element_type=jnp.float32).astype(jnp.bfloat16)
        marks = jnp.dot(logs[...], spread, preferred_element_type=jnp.float32)
        skip[0:1, pl.ds(start, part)] = marks[3:4] + marks[4:5] + marks[5:6]
        return state, marks.astype(jnp.bfloat16)

    for k in range(PARTS):
        for step in range(1, group):
            member = lax.rem(mine + step, group)
            start = pl.multiple_of(member * width + k * part, part)
            state, marks = local_state(start)
            s_ref[:rows, pl.ds(start, part)] = state
            s_ref[rows:, pl.ds(start, part)] = marks
            share(step, k).start()
    for k in range(PARTS):
        state, marks = local_state(pl.multiple_of(mine * width + k * part, part))
        got[0, :rows, pl.ds(k * part, part)] = state
        got[0, rows:, pl.ds(k * part, part)] = marks

    block = 8 * HEADDIM
    blocks = inner // block
    c_rows = act[:, inner + STATE : inner + 2 * STATE]
    scores = lax.dot_general(c_rows, b_rows, (((1,), (1,)), ((), ())), preferred_element_type=jnp.float32)
    lower = lax.broadcasted_iota(jnp.int32, (tokens, tokens), 0) >= lax.broadcasted_iota(jnp.int32, (tokens, tokens), 1)
    scores = jnp.where(lower, scores, 0.0)
    first = lax.broadcasted_iota(jnp.int32, (tokens, 2 * HEADDIM), 1) < HEADDIM

    def inside_block(g, carry):
        for pair in range(4):
            columns = pl.ds(pl.multiple_of(g * block + pair * 128, 128), 128)
            x = act[:, columns]
            stacked = jnp.concatenate([x, x], axis=0)
            halves = []
            for half in range(2):
                h = pair * 2 + half
                col = cols[g, :, h : h + 1]
                row = rows_ref[g, h : h + 1, :]
                inside = jnp.exp(jnp.where(lower, col - row, -1e30)) * scores * steps[g, h : h + 1, :]
                halves.append(
                    jnp.dot(
                        jnp.concatenate(split(inside), axis=1), stacked,
                        preferred_element_type=jnp.float32,
                    )
                )
            mixed[:, columns] = jnp.where(first, halves[0], halves[1]) + skip[0:1, columns] * x.astype(jnp.float32)
        return carry

    ahead = (blocks * plane) // max(planes - 1, 1)
    lax.fori_loop(0, ahead, inside_block, 0)

    slots = [lax.rem(mine - i + group, group) for i in range(group)]
    for k in range(PARTS):
        columns = pl.ds(k * part, part)
        for step in range(1, group):
            share(step, k).wait_recv()
        running = jnp.zeros((rows, part), jnp.float32)
        level = jnp.zeros((1, part), jnp.float32)
        levels = [level]
        for i in range(group):
            tail = got[slots[i], rows : rows + EXTRA, columns].astype(jnp.float32)
            step_log = tail[0:1] + tail[1:2] + tail[2:3]
            running = jnp.exp(step_log) * running + got[slots[i], :rows, columns].astype(jnp.float32)
            gsum[i, :, columns] = running
            level = level + step_log
            levels.append(level)

        @pl.when(has_prev)
        def _():
            chain(k).wait_recv()

        @pl.when(jnp.logical_not(has_prev))
        def _():
            ein[:, columns] = jnp.zeros((rows, part), jnp.bfloat16)

        entering = ein[:, columns].astype(jnp.float32)

        @pl.when(has_next)
        def _():
            eout[:, columns] = (jnp.exp(levels[group]) * entering + gsum[group - 1, :, columns]).astype(jnp.bfloat16)
            chain(k).start()

        for j in range(group):
            if j == 0:
                value = entering
            else:
                value = jnp.exp(levels[j]) * entering + gsum[j - 1, :, columns]
            fsend[lax.rem(j - mine + group, group), :, columns] = value.astype(jnp.bfloat16)
        for step in range(1, group):
            back(step, k).start()
        own = pl.ds(pl.multiple_of(mine * width + k * part, part), part)
        f_ref[:, own] = fsend[0, :, columns]

    lax.fori_loop(ahead, blocks, inside_block, 0)

    def outside(source, k):
        where = pl.multiple_of(source * width + k * part, part)
        outer = jnp.dot(c_rows, f_ref[:, pl.ds(where, part)], preferred_element_type=jnp.float32)
        for pair in range(part // 128):
            offset = (k * part) // HEADDIM + 2 * pair
            g, h = source * (width // block) + offset // 8, offset % 8
            columns = pl.ds(pl.multiple_of(where + pair * 128, 128), 128)
            level = jnp.where(first, cols[g, :, h : h + 1], cols[g, :, h + 1 : h + 2])
            total = mixed[:, columns] + jnp.exp(level) * outer[:, pair * 128 : pair * 128 + 128]
            z = gate[:, columns].astype(jnp.float32)
            gated = total.astype(jnp.bfloat16).astype(jnp.float32) * (z / (1.0 + jnp.exp(-z)))
            mixed[:, columns] = gated
            squares[...] += gated * gated

    squares[...] = jnp.zeros_like(squares)
    for k in range(PARTS):
        outside(mine, k)
        for step in range(1, group):
            source = lax.rem(mine - step + group, group)
            landed = pl.ds(pl.multiple_of(source * width + k * part, part), part)
            pltpu.make_async_remote_copy(
                src_ref=fsend.at[step, :, pl.ds(k * part, part)],
                dst_ref=f_ref.at[:, landed],
                send_sem=send_f.at[step, k],
                recv_sem=recv_f.at[step, k],
                device_id={"seq": base + lax.rem(mine + step, group)},
                device_id_type=MESH,
            ).wait_recv()
            outside(source, k)

    def norm(r, carry):
        take = pl.ds(pl.multiple_of(r * 16, 16), 16)
        mean = jnp.sum(squares[take, :], axis=-1, keepdims=True) * (1.0 / inner)
        out[take, :] = (mixed[take, :] * lax.rsqrt(mean + 1e-05) * gain[...]).astype(jnp.bfloat16)
        return carry

    lax.fori_loop(0, tokens // 16, norm, 0)

    @pl.when(me < count - 1)
    def _():
        hand_on.wait_send()

    for k in range(PARTS):
        for step in range(1, group):
            share(step, k).wait_send()
            back(step, k).wait_send()

        @pl.when(has_next)
        def _():
            chain(k).wait_send()


def mixer(tails, logs, conv_input, *others):
    count = lax.axis_size("seq")
    group = GROUP if count % GROUP == 0 else 1
    rows = STATE
    inner = HEADS * HEADDIM
    width = inner // group
    tokens = conv_input.shape[0]
    return pl.pallas_call(
        functools.partial(prefix_kernel, count, group),
        out_shape=jax.ShapeDtypeStruct((tokens, inner), jnp.bfloat16),
        in_specs=[pl.BlockSpec(memory_space=pltpu.VMEM)] * (3 + len(others)),
        out_specs=pl.BlockSpec(memory_space=pltpu.VMEM),
        scratch_shapes=[
            pltpu.VMEM(conv_input.shape, jnp.bfloat16),
            pltpu.VMEM((tokens + 8, conv_input.shape[1]), jnp.float32),
            pltpu.VMEM((EXTRA, conv_input.shape[1]), jnp.bfloat16),
            pltpu.VMEM((8, inner), jnp.float32),
            pltpu.VMEM((rows + EXTRA, inner), jnp.bfloat16),
            pltpu.VMEM((rows, inner), jnp.bfloat16),
            pltpu.VMEM((tokens, inner), jnp.float32),
            pltpu.VMEM((tokens, 128), jnp.float32),
            pltpu.VMEM((group, rows + EXTRA, width), jnp.bfloat16),
            pltpu.VMEM((rows, width), jnp.bfloat16),
            pltpu.VMEM((rows, width), jnp.bfloat16),
            pltpu.VMEM((group, rows, width), jnp.bfloat16),
            pltpu.VMEM((group, rows, width), jnp.float32),
            pltpu.SemaphoreType.DMA,
            pltpu.SemaphoreType.DMA,
            pltpu.SemaphoreType.DMA((group, PARTS)),
            pltpu.SemaphoreType.DMA((group, PARTS)),
            pltpu.SemaphoreType.DMA((PARTS,)),
            pltpu.SemaphoreType.DMA((PARTS,)),
            pltpu.SemaphoreType.DMA((group, PARTS)),
            pltpu.SemaphoreType.DMA((group, PARTS)),
        ],
        compiler_params=pltpu.CompilerParams(
            collective_id=0, has_side_effects=True, vmem_limit_bytes=40 * 1024 * 1024
        ),
    )(tails, logs, conv_input, *others)


def shards(
    conv_input, gate_input, step_input, conv_weight, convolution_bias,
    step_bias, decay_log, skip_gain, norm_gain,
):
    highest = lax.Precision.HIGHEST
    tokens = conv_input.shape[0]
    step_size = jax.nn.softplus(step_input.astype(jnp.float32) + step_bias[None, :])
    rate = -jnp.exp(decay_log)
    lower = (jnp.arange(tokens)[:, None] >= jnp.arange(tokens)[None, :]).astype(jnp.float32)
    within = jnp.dot(lower, step_size * rate[None, :], precision=highest)
    ends = within[-1]
    tail = jnp.exp(ends[None, :] - within) * step_size
    top = lax.reduce_precision(tail, 8, 7)
    tails = jnp.concatenate([top, tail - top], axis=1).astype(jnp.bfloat16)
    both = jnp.stack([ends, skip_gain])
    high = lax.reduce_precision(both, 8, 7)
    middle = lax.reduce_precision(both - high, 8, 7)
    low = lax.reduce_precision(both - high - middle, 8, 7)
    logs = jnp.transpose(jnp.stack([high, middle, low]), (1, 0, 2)).reshape(6, HEADS)
    logs = jnp.pad(logs, ((0, EXTRA - 6), (0, 0))).astype(jnp.bfloat16)
    logs = jnp.concatenate([logs, jnp.zeros_like(logs)], axis=1)
    groups = HEADS // 8
    cols = jnp.transpose(within.reshape(tokens, groups, 8), (1, 0, 2))
    rows = jnp.transpose(within).reshape(groups, 8, tokens)
    steps = jnp.transpose(step_size).reshape(groups, 8, tokens)
    return mixer(
        tails, logs, conv_input, conv_weight, convolution_bias[None, :], gate_input,
        cols, rows, steps, norm_gain[None, :],
    )


def solution(mesh):
    in_specs = (
        P(("doc", "seq"), None),
        P(("doc", "seq"), None),
        P(("doc", "seq"), None),
        P(), P(), P(), P(), P(), P(),
    )
    out_specs = P(("doc", "seq"), None)
    return jax.shard_map(shards, mesh=mesh, in_specs=in_specs, out_specs=out_specs, check_vma=False)
```

```python
import functools
import jax
import jax.numpy as jnp
from jax import lax
from jax.experimental import pallas as pl
from jax.experimental.pallas import tpu as pltpu
from jax.sharding import PartitionSpec as P

HEADDIM = 64
STATE = 128
HEADS = 64
GROUP = 4
PARTS = 8
EXTRA = 16
MESH = pl.DeviceIdType.MESH


def shifted(value, axis, steps):
    count = lax.axis_size(axis)
    initial, last = (max(0, -steps), min(count, count - steps))
    return lax.ppermute(value, axis, [(source, source + steps) for source in range(initial, last)])


def convolve(conv_input, conv_weight, convolution_bias):
    tap_count = conv_weight.shape[0]
    row_count = conv_input.shape[0]
    earlier = shifted(conv_input[row_count - (tap_count - 1) :], "seq", 1)
    padded = jnp.concatenate([earlier, conv_input], axis=0).astype(jnp.float32)
    mixed = convolution_bias[None, :]
    for offset in range(tap_count):
        mixed = mixed + conv_weight[offset][None, :] * padded[offset : offset + row_count]
    return jax.nn.silu(mixed).astype(jnp.bfloat16)


def split(value):
    high = value.astype(jnp.bfloat16)
    low = (value - high.astype(jnp.float32)).astype(jnp.bfloat16)
    return high, low


def prefix_kernel(
    count, group, tails, logs, act, gate, cols, rows_ref, steps, skip, gain,
    out, s_ref, f_ref, mixed, squares, got, ein, eout, fsend, gsum,
    send_a, recv_a, send_c, recv_c, send_f, recv_f,
):
    rows = ein.shape[0]
    width = ein.shape[1]
    part = width // PARTS
    planes = count // group
    me = lax.axis_index("seq")
    mine = lax.rem(me, group)
    plane = me // group
    base = plane * group
    has_prev = plane > 0
    has_next = plane < planes - 1
    before = jnp.maximum(me - group, 0)
    after = jnp.minimum(me + group, count - 1)

    barrier = pltpu.get_barrier_semaphore()
    for step in range(1, group):
        other = base + lax.rem(mine + step, group)
        pl.semaphore_signal(barrier, inc=1, device_id={"seq": other}, device_id_type=MESH)

    @pl.when(has_prev)
    def _():
        pl.semaphore_signal(barrier, inc=1, device_id={"seq": before}, device_id_type=MESH)

    @pl.when(has_next)
    def _():
        pl.semaphore_signal(barrier, inc=1, device_id={"seq": after}, device_id_type=MESH)

    peers = group - 1 + jnp.minimum(plane, 1) + jnp.minimum(planes - 1 - plane, 1)
    pl.semaphore_wait(barrier, peers)

    def share(step, k):
        member = lax.rem(mine + step, group)
        return pltpu.make_async_remote_copy(
            src_ref=s_ref.at[:, pl.ds(pl.multiple_of(member * width + k * part, part), part)],
            dst_ref=got.at[step, :, pl.ds(k * part, part)],
            send_sem=send_a.at[step, k],
            recv_sem=recv_a.at[step, k],
            device_id={"seq": base + member},
            device_id_type=MESH,
        )

    def chain(k):
        columns = pl.ds(k * part, part)
        return pltpu.make_async_remote_copy(
            src_ref=eout.at[:, columns],
            dst_ref=ein.at[:, columns],
            send_sem=send_c.at[k],
            recv_sem=recv_c.at[k],
            device_id={"seq": after},
            device_id_type=MESH,
        )

    def back(step, k):
        member = lax.rem(mine + step, group)
        own = pl.ds(pl.multiple_of(mine * width + k * part, part), part)
        return pltpu.make_async_remote_copy(
            src_ref=fsend.at[step, :, pl.ds(k * part, part)],
            dst_ref=f_ref.at[:, own],
            send_sem=send_f.at[step, k],
            recv_sem=recv_f.at[step, k],
            device_id={"seq": base + member},
            device_id_type=MESH,
        )

    inner = f_ref.shape[1]
    b_rows = act[:, inner : inner + STATE]
    turned = jnp.transpose(b_rows.astype(jnp.float32)).astype(jnp.bfloat16)
    factors = tails[...]
    lane = lax.broadcasted_iota(jnp.int32, (2 * HEADS, part), 1)
    head = lax.rem(lax.broadcasted_iota(jnp.int32, (2 * HEADS, part), 0), HEADS)

    def local_state(start):
        low = head * HEADDIM - start
        spread = jnp.where((lane >= low) & (lane < low + HEADDIM), 1.0, 0.0).astype(jnp.bfloat16)
        tail = jnp.dot(factors, spread, preferred_element_type=jnp.float32)
        weighted = (tail * act[:, pl.ds(start, part)].astype(jnp.float32)).astype(jnp.bfloat16)
        state = jnp.dot(turned, weighted, preferred_element_type=jnp.float32).astype(jnp.bfloat16)
        return state, jnp.dot(logs[...], spread, preferred_element_type=jnp.float32).astype(jnp.bfloat16)

    for k in range(PARTS):
        for step in range(1, group):
            member = lax.rem(mine + step, group)
            start = pl.multiple_of(member * width + k * part, part)
            state, marks = local_state(start)
            s_ref[:rows, pl.ds(start, part)] = state
            s_ref[rows:, pl.ds(start, part)] = marks
            share(step, k).start()
    for k in range(PARTS):
        state, marks = local_state(pl.multiple_of(mine * width + k * part, part))
        got[0, :rows, pl.ds(k * part, part)] = state
        got[0, rows:, pl.ds(k * part, part)] = marks

    tokens = act.shape[0]
    block = 8 * HEADDIM
    blocks = inner // block
    c_rows = act[:, inner + STATE : inner + 2 * STATE]
    scores = lax.dot_general(c_rows, b_rows, (((1,), (1,)), ((), ())), preferred_element_type=jnp.float32)
    lower = lax.broadcasted_iota(jnp.int32, (tokens, tokens), 0) >= lax.broadcasted_iota(jnp.int32, (tokens, tokens), 1)
    scores = jnp.where(lower, scores, 0.0)
    first = lax.broadcasted_iota(jnp.int32, (tokens, 2 * HEADDIM), 1) < HEADDIM

    def inside_block(g, carry):
        for pair in range(4):
            columns = pl.ds(pl.multiple_of(g * block + pair * 128, 128), 128)
            x = act[:, columns]
            stacked = jnp.concatenate([x, x], axis=0)
            halves = []
            for half in range(2):
                h = pair * 2 + half
                col = cols[g, :, h : h + 1]
                row = rows_ref[g, h : h + 1, :]
                inside = jnp.exp(jnp.where(lower, col - row, -1e30)) * scores * steps[g, h : h + 1, :]
                halves.append(
                    jnp.dot(
                        jnp.concatenate(split(inside), axis=1), stacked,
                        preferred_element_type=jnp.float32,
                    )
                )
            mixed[:, columns] = jnp.where(first, halves[0], halves[1]) + skip[:, columns] * x.astype(jnp.float32)
        return carry

    ahead = (blocks * plane) // max(planes - 1, 1)
    lax.fori_loop(0, ahead, inside_block, 0)

    slots = [lax.rem(mine - i + group, group) for i in range(group)]
    for k in range(PARTS):
        columns = pl.ds(k * part, part)
        for step in range(1, group):
            share(step, k).wait_recv()
        running = jnp.zeros((rows, part), jnp.float32)
        level = jnp.zeros((1, part), jnp.float32)
        levels = [level]
        for i in range(group):
            tail = got[slots[i], rows : rows + EXTRA, columns].astype(jnp.float32)
            step_log = tail[0:1] + tail[1:2] + tail[2:3]
            running = jnp.exp(step_log) * running + got[slots[i], :rows, columns].astype(jnp.float32)
            gsum[i, :, columns] = running
            level = level + step_log
            levels.append(level)

        @pl.when(has_prev)
        def _():
            chain(k).wait_recv()

        @pl.when(jnp.logical_not(has_prev))
        def _():
            ein[:, columns] = jnp.zeros((rows, part), jnp.bfloat16)

        entering = ein[:, columns].astype(jnp.float32)

        @pl.when(has_next)
        def _():
            eout[:, columns] = (jnp.exp(levels[group]) * entering + gsum[group - 1, :, columns]).astype(jnp.bfloat16)
            chain(k).start()

        for j in range(group):
            if j == 0:
                value = entering
            else:
                value = jnp.exp(levels[j]) * entering + gsum[j - 1, :, columns]
            fsend[lax.rem(j - mine + group, group), :, columns] = value.astype(jnp.bfloat16)
        for step in range(1, group):
            back(step, k).start()
        own = pl.ds(pl.multiple_of(mine * width + k * part, part), part)
        f_ref[:, own] = fsend[0, :, columns]

    lax.fori_loop(ahead, blocks, inside_block, 0)

    def outside(source, k):
        where = pl.multiple_of(source * width + k * part, part)
        outer = jnp.dot(c_rows, f_ref[:, pl.ds(where, part)], preferred_element_type=jnp.float32)
        for pair in range(part // 128):
            offset = (k * part) // HEADDIM + 2 * pair
            g, h = source * (width // block) + offset // 8, offset % 8
            columns = pl.ds(pl.multiple_of(where + pair * 128, 128), 128)
            level = jnp.where(first, cols[g, :, h : h + 1], cols[g, :, h + 1 : h + 2])
            total = mixed[:, columns] + jnp.exp(level) * outer[:, pair * 128 : pair * 128 + 128]
            z = gate[:, columns].astype(jnp.float32)
            gated = total.astype(jnp.bfloat16).astype(jnp.float32) * (z / (1.0 + jnp.exp(-z)))
            mixed[:, columns] = gated
            squares[...] += gated * gated

    squares[...] = jnp.zeros_like(squares)
    for k in range(PARTS):
        outside(mine, k)
        for step in range(1, group):
            source = lax.rem(mine - step + group, group)
            landed = pl.ds(pl.multiple_of(source * width + k * part, part), part)
            pltpu.make_async_remote_copy(
                src_ref=fsend.at[step, :, pl.ds(k * part, part)],
                dst_ref=f_ref.at[:, landed],
                send_sem=send_f.at[step, k],
                recv_sem=recv_f.at[step, k],
                device_id={"seq": base + lax.rem(mine + step, group)},
                device_id_type=MESH,
            ).wait_recv()
            outside(source, k)

    def norm(r, carry):
        take = pl.ds(pl.multiple_of(r * 16, 16), 16)
        mean = jnp.sum(squares[take, :], axis=-1, keepdims=True) * (1.0 / inner)
        out[take, :] = (mixed[take, :] * lax.rsqrt(mean + 1e-05) * gain[...]).astype(jnp.bfloat16)
        return carry

    lax.fori_loop(0, tokens // 16, norm, 0)

    for k in range(PARTS):
        for step in range(1, group):
            share(step, k).wait_send()
            back(step, k).wait_send()

        @pl.when(has_next)
        def _():
            chain(k).wait_send()


def mixer(tails, logs, activated, *others):
    count = lax.axis_size("seq")
    group = GROUP if count % GROUP == 0 else 1
    rows = STATE
    inner = HEADS * HEADDIM
    width = inner // group
    tokens = activated.shape[0]
    return pl.pallas_call(
        functools.partial(prefix_kernel, count, group),
        out_shape=jax.ShapeDtypeStruct((tokens, inner), jnp.bfloat16),
        in_specs=[pl.BlockSpec(memory_space=pltpu.VMEM)] * (3 + len(others)),
        out_specs=pl.BlockSpec(memory_space=pltpu.VMEM),
        scratch_shapes=[
            pltpu.VMEM((rows + EXTRA, inner), jnp.bfloat16),
            pltpu.VMEM((rows, inner), jnp.bfloat16),
            pltpu.VMEM((tokens, inner), jnp.float32),
            pltpu.VMEM((tokens, 128), jnp.float32),
            pltpu.VMEM((group, rows + EXTRA, width), jnp.bfloat16),
            pltpu.VMEM((rows, width), jnp.bfloat16),
            pltpu.VMEM((rows, width), jnp.bfloat16),
            pltpu.VMEM((group, rows, width), jnp.bfloat16),
            pltpu.VMEM((group, rows, width), jnp.float32),
            pltpu.SemaphoreType.DMA((group, PARTS)),
            pltpu.SemaphoreType.DMA((group, PARTS)),
            pltpu.SemaphoreType.DMA((PARTS,)),
            pltpu.SemaphoreType.DMA((PARTS,)),
            pltpu.SemaphoreType.DMA((group, PARTS)),
            pltpu.SemaphoreType.DMA((group, PARTS)),
        ],
        compiler_params=pltpu.CompilerParams(
            collective_id=0, has_side_effects=True, vmem_limit_bytes=32 * 1024 * 1024
        ),
    )(tails, logs, activated, *others)


def shards(
    conv_input, gate_input, step_input, conv_weight, convolution_bias,
    step_bias, decay_log, skip_gain, norm_gain,
):
    highest = lax.Precision.HIGHEST
    inner = HEADS * HEADDIM
    tokens = conv_input.shape[0]
    activated = convolve(conv_input, conv_weight, convolution_bias)
    step_size = jax.nn.softplus(step_input.astype(jnp.float32) + step_bias[None, :])
    rate = -jnp.exp(decay_log)
    lower = (jnp.arange(tokens)[:, None] >= jnp.arange(tokens)[None, :]).astype(jnp.float32)
    within = jnp.dot(lower, step_size * rate[None, :], precision=highest)
    ends = within[-1]
    tail = jnp.exp(ends[None, :] - within) * step_size
    top = lax.reduce_precision(tail, 8, 7)
    tails = jnp.concatenate([top, tail - top], axis=1).astype(jnp.bfloat16)
    high = lax.reduce_precision(ends, 8, 7)
    middle = lax.reduce_precision(ends - high, 8, 7)
    low = lax.reduce_precision(ends - high - middle, 8, 7)
    logs = jnp.stack([high, middle, low] + [jnp.zeros_like(low)] * (EXTRA - 3)).astype(jnp.bfloat16)
    logs = jnp.concatenate([logs, jnp.zeros_like(logs)], axis=1)
    groups = HEADS // 8
    cols = jnp.transpose(within.reshape(tokens, groups, 8), (1, 0, 2))
    rows = jnp.transpose(within).reshape(groups, 8, tokens)
    steps = jnp.transpose(step_size).reshape(groups, 8, tokens)
    skip = jnp.repeat(skip_gain, HEADDIM)[None, :]
    return mixer(tails, logs, activated, gate_input, cols, rows, steps, skip, norm_gain[None, :])


def solution(mesh):
    in_specs = (
        P(("doc", "seq"), None),
        P(("doc", "seq"), None),
        P(("doc", "seq"), None),
        P(), P(), P(), P(), P(), P(),
    )
    out_specs = P(("doc", "seq"), None)
    return jax.shard_map(shards, mesh=mesh, in_specs=in_specs, out_specs=out_specs, check_vma=False)
```

```python
import functools
import jax
import jax.numpy as jnp
from jax import lax
from jax.experimental import pallas as pl
from jax.experimental.pallas import tpu as pltpu
from jax.sharding import PartitionSpec as P

HEADDIM = 64
STATE = 128
HEADS = 64
GROUP = 4
PARTS = 8
EXTRA = 16
MESH = pl.DeviceIdType.MESH


def shifted(value, axis, steps):
    count = lax.axis_size(axis)
    initial, last = (max(0, -steps), min(count, count - steps))
    return lax.ppermute(value, axis, [(source, source + steps) for source in range(initial, last)])


def convolve(conv_input, conv_weight, convolution_bias):
    tap_count = conv_weight.shape[0]
    row_count = conv_input.shape[0]
    earlier = shifted(conv_input[row_count - (tap_count - 1) :], "seq", 1)
    padded = jnp.concatenate([earlier, conv_input], axis=0).astype(jnp.float32)
    mixed = convolution_bias[None, :]
    for offset in range(tap_count):
        mixed = mixed + conv_weight[offset][None, :] * padded[offset : offset + row_count]
    return jax.nn.silu(mixed).astype(jnp.bfloat16)


def split(value):
    high = value.astype(jnp.bfloat16)
    low = (value - high.astype(jnp.float32)).astype(jnp.bfloat16)
    return high, low


def prefix_kernel(
    count, group, tails, logs, act, gate, cols, rows_ref, steps, gain,
    out, skip, s_ref, f_ref, mixed, squares, got, ein, eout, fsend, gsum,
    send_a, recv_a, send_c, recv_c, send_f, recv_f,
):
    rows = ein.shape[0]
    width = ein.shape[1]
    part = width // PARTS
    planes = count // group
    me = lax.axis_index("seq")
    mine = lax.rem(me, group)
    plane = me // group
    base = plane * group
    has_prev = plane > 0
    has_next = plane < planes - 1
    before = jnp.maximum(me - group, 0)
    after = jnp.minimum(me + group, count - 1)

    barrier = pltpu.get_barrier_semaphore()
    for step in range(1, group):
        other = base + lax.rem(mine + step, group)
        pl.semaphore_signal(barrier, inc=1, device_id={"seq": other}, device_id_type=MESH)

    @pl.when(has_prev)
    def _():
        pl.semaphore_signal(barrier, inc=1, device_id={"seq": before}, device_id_type=MESH)

    @pl.when(has_next)
    def _():
        pl.semaphore_signal(barrier, inc=1, device_id={"seq": after}, device_id_type=MESH)

    peers = group - 1 + jnp.minimum(plane, 1) + jnp.minimum(planes - 1 - plane, 1)
    pl.semaphore_wait(barrier, peers)

    def share(step, k):
        member = lax.rem(mine + step, group)
        return pltpu.make_async_remote_copy(
            src_ref=s_ref.at[:, pl.ds(pl.multiple_of(member * width + k * part, part), part)],
            dst_ref=got.at[step, :, pl.ds(k * part, part)],
            send_sem=send_a.at[step, k],
            recv_sem=recv_a.at[step, k],
            device_id={"seq": base + member},
            device_id_type=MESH,
        )

    def chain(k):
        columns = pl.ds(k * part, part)
        return pltpu.make_async_remote_copy(
            src_ref=eout.at[:, columns],
            dst_ref=ein.at[:, columns],
            send_sem=send_c.at[k],
            recv_sem=recv_c.at[k],
            device_id={"seq": after},
            device_id_type=MESH,
        )

    def back(step, k):
        member = lax.rem(mine + step, group)
        own = pl.ds(pl.multiple_of(mine * width + k * part, part), part)
        return pltpu.make_async_remote_copy(
            src_ref=fsend.at[step, :, pl.ds(k * part, part)],
            dst_ref=f_ref.at[:, own],
            send_sem=send_f.at[step, k],
            recv_sem=recv_f.at[step, k],
            device_id={"seq": base + member},
            device_id_type=MESH,
        )

    inner = f_ref.shape[1]
    b_rows = act[:, inner : inner + STATE]
    turned = jnp.transpose(b_rows.astype(jnp.float32)).astype(jnp.bfloat16)
    factors = tails[...]
    lane = lax.broadcasted_iota(jnp.int32, (2 * HEADS, part), 1)
    head = lax.rem(lax.broadcasted_iota(jnp.int32, (2 * HEADS, part), 0), HEADS)

    def local_state(start):
        low = head * HEADDIM - start
        spread = jnp.where((lane >= low) & (lane < low + HEADDIM), 1.0, 0.0).astype(jnp.bfloat16)
        tail = jnp.dot(factors, spread, preferred_element_type=jnp.float32)
        weighted = (tail * act[:, pl.ds(start, part)].astype(jnp.float32)).astype(jnp.bfloat16)
        state = jnp.dot(turned, weighted, preferred_element_type=jnp.float32).astype(jnp.bfloat16)
        marks = jnp.dot(logs[...], spread, preferred_element_type=jnp.float32)
        skip[0:1, pl.ds(start, part)] = marks[3:4] + marks[4:5] + marks[5:6]
        return state, marks.astype(jnp.bfloat16)

    for k in range(PARTS):
        for step in range(1, group):
            member = lax.rem(mine + step, group)
            start = pl.multiple_of(member * width + k * part, part)
            state, marks = local_state(start)
            s_ref[:rows, pl.ds(start, part)] = state
            s_ref[rows:, pl.ds(start, part)] = marks
            share(step, k).start()
    for k in range(PARTS):
        state, marks = local_state(pl.multiple_of(mine * width + k * part, part))
        got[0, :rows, pl.ds(k * part, part)] = state
        got[0, rows:, pl.ds(k * part, part)] = marks

    tokens = act.shape[0]
    block = 8 * HEADDIM
    blocks = inner // block
    c_rows = act[:, inner + STATE : inner + 2 * STATE]
    scores = lax.dot_general(c_rows, b_rows, (((1,), (1,)), ((), ())), preferred_element_type=jnp.float32)
    lower = lax.broadcasted_iota(jnp.int32, (tokens, tokens), 0) >= lax.broadcasted_iota(jnp.int32, (tokens, tokens), 1)
    scores = jnp.where(lower, scores, 0.0)
    first = lax.broadcasted_iota(jnp.int32, (tokens, 2 * HEADDIM), 1) < HEADDIM

    def inside_block(g, carry):
        for pair in range(4):
            columns = pl.ds(pl.multiple_of(g * block + pair * 128, 128), 128)
            x = act[:, columns]
            stacked = jnp.concatenate([x, x], axis=0)
            halves = []
            for half in range(2):
                h = pair * 2 + half
                col = cols[g, :, h : h + 1]
                row = rows_ref[g, h : h + 1, :]
                inside = jnp.exp(jnp.where(lower, col - row, -1e30)) * scores * steps[g, h : h + 1, :]
                halves.append(
                    jnp.dot(
                        jnp.concatenate(split(inside), axis=1), stacked,
                        preferred_element_type=jnp.float32,
                    )
                )
            mixed[:, columns] = jnp.where(first, halves[0], halves[1]) + skip[0:1, columns] * x.astype(jnp.float32)
        return carry

    ahead = (blocks * plane) // max(planes - 1, 1)
    lax.fori_loop(0, ahead, inside_block, 0)

    slots = [lax.rem(mine - i + group, group) for i in range(group)]
    for k in range(PARTS):
        columns = pl.ds(k * part, part)
        for step in range(1, group):
            share(step, k).wait_recv()
        running = jnp.zeros((rows, part), jnp.float32)
        level = jnp.zeros((1, part), jnp.float32)
        levels = [level]
        for i in range(group):
            tail = got[slots[i], rows : rows + EXTRA, columns].astype(jnp.float32)
            step_log = tail[0:1] + tail[1:2] + tail[2:3]
            running = jnp.exp(step_log) * running + got[slots[i], :rows, columns].astype(jnp.float32)
            gsum[i, :, columns] = running
            level = level + step_log
            levels.append(level)

        @pl.when(has_prev)
        def _():
            chain(k).wait_recv()

        @pl.when(jnp.logical_not(has_prev))
        def _():
            ein[:, columns] = jnp.zeros((rows, part), jnp.bfloat16)

        entering = ein[:, columns].astype(jnp.float32)

        @pl.when(has_next)
        def _():
            eout[:, columns] = (jnp.exp(levels[group]) * entering + gsum[group - 1, :, columns]).astype(jnp.bfloat16)
            chain(k).start()

        for j in range(group):
            if j == 0:
                value = entering
            else:
                value = jnp.exp(levels[j]) * entering + gsum[j - 1, :, columns]
            fsend[lax.rem(j - mine + group, group), :, columns] = value.astype(jnp.bfloat16)
        for step in range(1, group):
            back(step, k).start()
        own = pl.ds(pl.multiple_of(mine * width + k * part, part), part)
        f_ref[:, own] = fsend[0, :, columns]

    lax.fori_loop(ahead, blocks, inside_block, 0)

    def outside(source, k):
        where = pl.multiple_of(source * width + k * part, part)
        outer = jnp.dot(c_rows, f_ref[:, pl.ds(where, part)], preferred_element_type=jnp.float32)
        for pair in range(part // 128):
            offset = (k * part) // HEADDIM + 2 * pair
            g, h = source * (width // block) + offset // 8, offset % 8
            columns = pl.ds(pl.multiple_of(where + pair * 128, 128), 128)
            level = jnp.where(first, cols[g, :, h : h + 1], cols[g, :, h + 1 : h + 2])
            total = mixed[:, columns] + jnp.exp(level) * outer[:, pair * 128 : pair * 128 + 128]
            z = gate[:, columns].astype(jnp.float32)
            gated = total.astype(jnp.bfloat16).astype(jnp.float32) * (z / (1.0 + jnp.exp(-z)))
            mixed[:, columns] = gated
            squares[...] += gated * gated

    squares[...] = jnp.zeros_like(squares)
    for k in range(PARTS):
        outside(mine, k)
        for step in range(1, group):
            source = lax.rem(mine - step + group, group)
            landed = pl.ds(pl.multiple_of(source * width + k * part, part), part)
            pltpu.make_async_remote_copy(
                src_ref=fsend.at[step, :, pl.ds(k * part, part)],
                dst_ref=f_ref.at[:, landed],
                send_sem=send_f.at[step, k],
                recv_sem=recv_f.at[step, k],
                device_id={"seq": base + lax.rem(mine + step, group)},
                device_id_type=MESH,
            ).wait_recv()
            outside(source, k)

    def norm(r, carry):
        take = pl.ds(pl.multiple_of(r * 16, 16), 16)
        mean = jnp.sum(squares[take, :], axis=-1, keepdims=True) * (1.0 / inner)
        out[take, :] = (mixed[take, :] * lax.rsqrt(mean + 1e-05) * gain[...]).astype(jnp.bfloat16)
        return carry

    lax.fori_loop(0, tokens // 16, norm, 0)

    for k in range(PARTS):
        for step in range(1, group):
            share(step, k).wait_send()
            back(step, k).wait_send()

        @pl.when(has_next)
        def _():
            chain(k).wait_send()


def mixer(tails, logs, activated, *others):
    count = lax.axis_size("seq")
    group = GROUP if count % GROUP == 0 else 1
    rows = STATE
    inner = HEADS * HEADDIM
    width = inner // group
    tokens = activated.shape[0]
    return pl.pallas_call(
        functools.partial(prefix_kernel, count, group),
        out_shape=jax.ShapeDtypeStruct((tokens, inner), jnp.bfloat16),
        in_specs=[pl.BlockSpec(memory_space=pltpu.VMEM)] * (3 + len(others)),
        out_specs=pl.BlockSpec(memory_space=pltpu.VMEM),
        scratch_shapes=[
            pltpu.VMEM((8, inner), jnp.float32),
            pltpu.VMEM((rows + EXTRA, inner), jnp.bfloat16),
            pltpu.VMEM((rows, inner), jnp.bfloat16),
            pltpu.VMEM((tokens, inner), jnp.float32),
            pltpu.VMEM((tokens, 128), jnp.float32),
            pltpu.VMEM((group, rows + EXTRA, width), jnp.bfloat16),
            pltpu.VMEM((rows, width), jnp.bfloat16),
            pltpu.VMEM((rows, width), jnp.bfloat16),
            pltpu.VMEM((group, rows, width), jnp.bfloat16),
            pltpu.VMEM((group, rows, width), jnp.float32),
            pltpu.SemaphoreType.DMA((group, PARTS)),
            pltpu.SemaphoreType.DMA((group, PARTS)),
            pltpu.SemaphoreType.DMA((PARTS,)),
            pltpu.SemaphoreType.DMA((PARTS,)),
            pltpu.SemaphoreType.DMA((group, PARTS)),
            pltpu.SemaphoreType.DMA((group, PARTS)),
        ],
        compiler_params=pltpu.CompilerParams(
            collective_id=0, has_side_effects=True, vmem_limit_bytes=32 * 1024 * 1024
        ),
    )(tails, logs, activated, *others)


def shards(
    conv_input, gate_input, step_input, conv_weight, convolution_bias,
    step_bias, decay_log, skip_gain, norm_gain,
):
    highest = lax.Precision.HIGHEST
    inner = HEADS * HEADDIM
    tokens = conv_input.shape[0]
    activated = convolve(conv_input, conv_weight, convolution_bias)
    step_size = jax.nn.softplus(step_input.astype(jnp.float32) + step_bias[None, :])
    rate = -jnp.exp(decay_log)
    lower = (jnp.arange(tokens)[:, None] >= jnp.arange(tokens)[None, :]).astype(jnp.float32)
    within = jnp.dot(lower, step_size * rate[None, :], precision=highest)
    ends = within[-1]
    tail = jnp.exp(ends[None, :] - within) * step_size
    top = lax.reduce_precision(tail, 8, 7)
    tails = jnp.concatenate([top, tail - top], axis=1).astype(jnp.bfloat16)
    both = jnp.stack([ends, skip_gain])
    high = lax.reduce_precision(both, 8, 7)
    middle = lax.reduce_precision(both - high, 8, 7)
    low = lax.reduce_precision(both - high - middle, 8, 7)
    logs = jnp.transpose(jnp.stack([high, middle, low]), (1, 0, 2)).reshape(6, HEADS)
    logs = jnp.pad(logs, ((0, EXTRA - 6), (0, 0))).astype(jnp.bfloat16)
    logs = jnp.concatenate([logs, jnp.zeros_like(logs)], axis=1)
    groups = HEADS // 8
    cols = jnp.transpose(within.reshape(tokens, groups, 8), (1, 0, 2))
    rows = jnp.transpose(within).reshape(groups, 8, tokens)
    steps = jnp.transpose(step_size).reshape(groups, 8, tokens)
    return mixer(tails, logs, activated, gate_input, cols, rows, steps, norm_gain[None, :])


def solution(mesh):
    in_specs = (
        P(("doc", "seq"), None),
        P(("doc", "seq"), None),
        P(("doc", "seq"), None),
        P(), P(), P(), P(), P(), P(),
    )
    out_specs = P(("doc", "seq"), None)
    return jax.shard_map(shards, mesh=mesh, in_specs=in_specs, out_specs=out_specs, check_vma=False)
```
